32 devices in a mesh: tp: 2 (over y), lat: 16 (over z, x, core).
Axes of the slice: x: 2, y: 2, z: 4, core: 2. Of those that a mesh axis runs over, the one named last changes fastest.
Arguments:
- queries: bfloat16 [256, 2048], P('lat', 'tp'), may hold values from -6 to 6
- key_cache: bfloat16 [256, 256, 1024], P('lat', None, 'tp'), may hold values from -6 to 6
- value_cache: bfloat16 [256, 256, 1024], P('lat', None, 'tp'), may hold values from -6 to 6
- new_key: bfloat16 [256, 1024], P('lat', 'tp'), may hold values from -6 to 6
- new_value: bfloat16 [256, 1024], P('lat', 'tp'), may hold values from -6 to 6
- lengths: int32 [256], P('lat'), may hold values from 1 to 256, as said below
- out_proj: bfloat16 [2048, 4608], P('tp', 'lat'), may hold values from -0.125 to 0.125
- residual: bfloat16 [256, 4608], P(None, 'lat'), may hold values from -3 to 3
- enc_weight: bfloat16 [4608, 8192], P(None, ('tp', 'lat')), may hold values from -0.1875 to 0.1875
- enc_bias: float32 [8192], P(('tp', 'lat')), may hold values from -1.5 to 1.5
- threshold_code: int32 [8192], P(('tp', 'lat')), may hold values from 0 to 15
- probe_weight: bfloat16 [8192, 256], P(('tp', 'lat')), may hold values from -0.0625 to 0.0625
- probe_bias: float32 [256], replicated, may hold values from -2.5 to 2.5
- head_weight: float32 [256, 16], replicated, may hold values from -0.375 to 0.375
- head_bias: float32 [16], replicated, may hold values from -2.5 to 2.5
Outputs:
- probe_scores: float32 [256, 256], P(('tp', 'lat'))
- harm_logits: float32 [256, 16], P(('tp', 'lat'))
The draws below stay inside these ranges and needn't reach their ends.
Inputs may be any that keep to these rules, and one draw needn't show every extreme that they name: `lengths`: some row has all 256 positions live.
All inputs are finite; a program needn't handle non-finite values.
Results may differ from the reference program's by a relative error of at most 0.0075.
Values may be sent and summed in bfloat16 or wider, within the bound.
No kernel may reach another device: no remote copies, remote signals or barrier semaphores. Data moves between devices by JAX's collectives and lax.ppermute only.
A program may use at most 64 MiB of HBM per device.

```python
import jax
import jax.numpy as jnp
from jax import lax

D = 4608
HEAD = 128
QHEADS = 16
KVHEADS = 8
PROBE = 256
CLASSES = 16
CACHE = 256
ROWS = 256
LATENTS = 8192


def draw_lengths(key, part):
    first, second = jax.random.split(key)
    drawn = jax.random.randint(first, (ROWS,), 1, CACHE + 1)
    chosen = jax.random.randint(second, (), 0, ROWS)
    return jnp.where(jnp.arange(ROWS) == chosen, CACHE, drawn).astype(jnp.int32)


def plant(values, key, least, largest):
    dims = values.shape
    index_at = [jax.random.randint(jax.random.fold_in(key, axis), (), 0, dims[axis]) for axis in range(len(dims))]
    values = values.at[tuple(index_at)].set(least)
    longest = dims.index(max(dims))
    index_at[longest] = (index_at[longest] + 1) % dims[longest]
    return values.at[tuple(index_at)].set(largest)


def block_scale(stream_key, dims, shards, low, high):
    loudness, own = 1.0, jax.random.fold_in(stream_key, 6)
    for axis_at, shards_of in shards:
        heights = jnp.exp(jax.random.uniform(jax.random.fold_in(own, axis_at), (shards_of,), jnp.float32, low / len(shards), high / len(shards)))
        loudness = loudness * jnp.repeat(heights, dims[axis_at] // shards_of).reshape([-1 if axis == axis_at else 1 for axis in range(len(dims))])
    return loudness


def centred(stream_key, dims, spread, reach, pieces=(), kind=jnp.bfloat16):
    values = jax.random.normal(stream_key, dims, jnp.float32) * spread
    if len(pieces) > 0:
        values = block_scale(stream_key, dims, pieces, -0.22, 0.18) * values
    return jnp.clip(values, min=-reach, max=reach).astype(kind)


def setup_inputs(seed: int = 0) -> dict:
    keys = jax.random.split(jax.random.key(seed), 16)
    return {
        "queries": centred(keys[0], (ROWS, QHEADS * HEAD), 1.0, 6.0, ((0, 16), (1, 2))),
        "key_cache": centred(keys[1], (ROWS, CACHE, KVHEADS * HEAD), 1.0, 6.0, ((0, 16), (2, 2))),
        "value_cache": centred(keys[2], (ROWS, CACHE, KVHEADS * HEAD), 1.0, 6.0, ((0, 16), (2, 2))),
        "new_key": centred(keys[3], (ROWS, KVHEADS * HEAD), 1.0, 6.0, ((0, 16), (1, 2))),
        "new_value": centred(keys[4], (ROWS, KVHEADS * HEAD), 1.0, 6.0, ((0, 16), (1, 2))),
        "lengths": draw_lengths(jax.random.fold_in(keys[15], 71), 0),
        "out_proj": centred(keys[6], (QHEADS * HEAD, D), (QHEADS * HEAD) ** -0.5, 0.125, ((0, 2), (1, 16))),
        "residual": centred(keys[7], (ROWS, D), 0.5, 3.0, ((1, 16),)),
        "enc_weight": centred(keys[8], (D, LATENTS), (D // 4) ** -0.5, 0.1875, ((1, 32),)),
        "enc_bias": centred(keys[9], (LATENTS,), 0.3, 1.5, ((0, 32),), jnp.float32),
        "threshold_code": plant(jax.random.randint(keys[10], (LATENTS,), 0, 16), jax.random.fold_in(keys[10], 1), 0, 15).astype(jnp.int32),
        "probe_weight": centred(keys[11], (LATENTS, PROBE), LATENTS ** -0.5, 0.0625, ((0, 32),)),
        "probe_bias": centred(keys[12], (PROBE,), 0.5, 2.5, (), jnp.float32),
        "head_weight": centred(keys[13], (PROBE, CLASSES), PROBE ** -0.5, 0.375, (), jnp.float32),
        "head_bias": centred(keys[14], (CLASSES,), 0.5, 2.5, (), jnp.float32),
    }


SOFT_CAP = 50.0
QUERY_SCALE = 1.0 / 12.0
RAMP_WIDTH = 0.25


def attend(queries, key_cache, value_cache, new_key, new_value, lengths):
    row_count, positions, kv_width = key_cache.shape
    kv_heads = kv_width // HEAD
    group_size = queries.shape[1] // kv_width
    grouped = queries.reshape(row_count, kv_heads, group_size, HEAD).astype(jnp.float32)
    key_rows = key_cache.reshape(row_count, positions, kv_heads, HEAD).astype(jnp.float32)
    values = value_cache.reshape(row_count, positions, kv_heads, HEAD).astype(jnp.float32)
    fresh_key = new_key.reshape(row_count, kv_heads, HEAD).astype(jnp.float32)
    fresh_value = new_value.reshape(row_count, kv_heads, 1, HEAD).astype(jnp.float32)
    cached = jnp.einsum("rkgd,rlkd->rkgl", grouped, key_rows)
    own_score = jnp.einsum("rkgd,rkd->rkg", grouped, fresh_key)
    cached = SOFT_CAP * jnp.tanh(cached * (QUERY_SCALE / SOFT_CAP))
    own_score = SOFT_CAP * jnp.tanh(own_score * (QUERY_SCALE / SOFT_CAP))
    live_mask = jnp.arange(positions, dtype=jnp.int32)[None, :] < lengths[:, None]
    cached_exp = jnp.where(live_mask[:, None, None, :], jnp.exp(cached), 0.0)
    own_exp = jnp.exp(own_score)
    denominator = jnp.sum(cached_exp, axis=-1) + own_exp
    cached_weight = (cached_exp / denominator[..., None]).astype(jnp.bfloat16)
    own_weight = (own_exp / denominator).astype(jnp.bfloat16)
    mixture = jnp.einsum("rkgl,rlkd->rkgd", cached_weight.astype(jnp.float32), values)
    mixture = mixture + own_weight.astype(jnp.float32)[..., None] * fresh_value
    return mixture.reshape(row_count, kv_heads * group_size * HEAD).astype(jnp.bfloat16)


def reference(queries, key_cache, value_cache, new_key, new_value, lengths, out_proj, residual, enc_weight, enc_bias, threshold_code, probe_weight, probe_bias, head_weight, head_bias):
    block_count = ROWS // 64

    def attend_block(items):
        return attend(items[0], items[1], items[2], items[3], items[4], items[5])

    stacked = (
        queries.reshape(block_count, 64, queries.shape[1]),
        key_cache.reshape(block_count, 64, CACHE, key_cache.shape[2]),
        value_cache.reshape(block_count, 64, CACHE, value_cache.shape[2]),
        new_key.reshape(block_count, 64, new_key.shape[1]),
        new_value.reshape(block_count, 64, new_value.shape[1]),
        lengths.reshape(block_count, 64),
    )
    attended = lax.map(attend_block, stacked).reshape(ROWS, QHEADS * HEAD)
    projected = jnp.dot(attended, out_proj, preferred_element_type=jnp.float32)
    stream = (residual.astype(jnp.float32) + projected).astype(jnp.bfloat16)
    lat_block = min(LATENTS, 2048)
    steps_count = LATENTS // lat_block

    def encode_block(carried, block_index):
        offset = (block_index * lat_block).astype(jnp.int32)
        weights = lax.dynamic_slice_in_dim(enc_weight, offset, lat_block, 1)
        bias_block = lax.dynamic_slice_in_dim(enc_bias, offset, lat_block, 0)
        code_block = lax.dynamic_slice_in_dim(threshold_code, offset, lat_block, 0)
        readout = lax.dynamic_slice_in_dim(probe_weight, offset, lat_block, 0)
        pre_act = jnp.dot(stream, weights, preferred_element_type=jnp.float32) + bias_block
        threshold = code_block.astype(jnp.float32) / 16.0
        ramped = jnp.clip((pre_act - threshold) / RAMP_WIDTH, 0.0, 1.0)
        activations = (pre_act * ramped).astype(jnp.bfloat16)
        return carried + jnp.dot(activations, readout, preferred_element_type=jnp.float32), None

    summed, _ = lax.scan(encode_block, jnp.zeros((ROWS, PROBE), jnp.float32), jnp.arange(steps_count, dtype=jnp.int32))
    probe_scores = summed + probe_bias
    harm_logits = jnp.dot(jax.nn.silu(probe_scores), head_weight, precision=lax.Precision.HIGHEST, preferred_element_type=jnp.float32) + head_bias
    return probe_scores, harm_logits
```

```python
import jax
import jax.numpy as jnp
from jax import lax
from jax.experimental import pallas as pl
from jax.experimental.pallas import tpu as pltpu
from jax.sharding import Mesh, PartitionSpec as P

HEAD = 128


SOFT_CAP = 50.0
QUERY_SCALE = 1.0 / 12.0
RAMP_WIDTH = 0.25

ALL = ("y", "z", "x", "c")
PLANE = ("y", "z", "x")


def attend(queries, key_cache, value_cache, new_key, new_value, lengths):
    row_count, positions, kv_width = key_cache.shape
    kv_heads = kv_width // HEAD
    group_size = queries.shape[1] // kv_width
    grouped = queries.reshape(row_count, kv_heads, group_size, HEAD)
    key_rows = key_cache.reshape(row_count, positions, kv_heads, HEAD)
    values = value_cache.reshape(row_count, positions, kv_heads, HEAD)
    fresh_key = new_key.reshape(row_count, kv_heads, HEAD)
    fresh_value = new_value.reshape(row_count, kv_heads, 1, HEAD).astype(jnp.float32)
    cached = jnp.einsum("rkgd,rlkd->rkgl", grouped, key_rows, preferred_element_type=jnp.float32)
    own_score = jnp.einsum("rkgd,rkd->rkg", grouped, fresh_key, preferred_element_type=jnp.float32)
    cached = SOFT_CAP * jnp.tanh(cached * (QUERY_SCALE / SOFT_CAP))
    own_score = SOFT_CAP * jnp.tanh(own_score * (QUERY_SCALE / SOFT_CAP))
    live_mask = jnp.arange(positions, dtype=jnp.int32)[None, :] < lengths[:, None]
    cached_exp = jnp.where(live_mask[:, None, None, :], jnp.exp(cached), 0.0)
    own_exp = jnp.exp(own_score)
    denominator = jnp.sum(cached_exp, axis=-1) + own_exp
    cached_weight = (cached_exp / denominator[..., None]).astype(jnp.bfloat16)
    own_weight = (own_exp / denominator).astype(jnp.bfloat16)
    mixture = jnp.einsum(
        "rkgl,rlkd->rkgd", cached_weight, values, preferred_element_type=jnp.float32
    )
    mixture = mixture + own_weight.astype(jnp.float32)[..., None] * fresh_value
    return mixture.reshape(row_count, kv_heads * group_size * HEAD).astype(jnp.bfloat16)


def xor(value, bits):
    return lax.ppermute(value, ALL, [(i, i ^ bits) for i in range(32)])


def encode_kernel(
    g00, g01, g10, g11, enc_own, enc_other, bias, threshold, probe_own, probe_other, out_ref, ordered
):
    z, x = lax.axis_index("z"), lax.axis_index("x")
    pieces = ((g00, g10), (g01, g11))
    block = g00.shape[2]
    pre_own = jnp.zeros((2 * g00.shape[1], enc_own.shape[1]), jnp.float32)
    pre_other = pre_own
    for dx in range(2):
        for dz in range(4):
            start = pl.multiple_of(((z ^ dz) * 2 + (x ^ dx)) * block, block)
            rows = jnp.concatenate([pieces[dx][0][dz], pieces[dx][1][dz]], axis=0)
            pre_own += jnp.dot(rows, enc_own[pl.ds(start, block), :], preferred_element_type=jnp.float32)
            pre_other += jnp.dot(rows, enc_other[pl.ds(start, block), :], preferred_element_type=jnp.float32)

    def activate(pre, at):
        pre = pre + bias[at : at + 1, :]
        ramped = jnp.clip((pre - threshold[at : at + 1, :]) / RAMP_WIDTH, 0.0, 1.0)
        return (pre * ramped).astype(jnp.bfloat16)

    partial = jnp.dot(activate(pre_own, 0), probe_own[...], preferred_element_type=jnp.float32)
    partial += jnp.dot(activate(pre_other, 1), probe_other[...], preferred_element_type=jnp.float32)
    for half in range(2):
        for b in range(16):
            at = half * 64 + b * 4
            ordered[b, 4 * half : 4 * half + 4, :] = partial[at : at + 4, :]
    out_ref[...] = ordered[...].astype(jnp.bfloat16)


def vmem(count):
    return [pl.BlockSpec(memory_space=pltpu.VMEM)] * count


def encode(gathered, enc, bias, threshold, probe):
    columns = probe[0].shape[1]
    return pl.pallas_call(
        encode_kernel,
        out_shape=jax.ShapeDtypeStruct((16, 8, columns), jnp.bfloat16),
        in_specs=vmem(10),
        out_specs=pl.BlockSpec(memory_space=pltpu.VMEM),
        scratch_shapes=[pltpu.VMEM((16, 8, columns), jnp.float32)],
        compiler_params=pltpu.CompilerParams(vmem_limit_bytes=32 * 1024 * 1024),
        name="encode",
    )(*gathered, *enc, bias, threshold, *probe)


def finish_kernel(parts, probe_bias, head_weight, head_bias, scores_ref, logits_ref):
    sums = parts[...].astype(jnp.float32)
    first = jnp.sum(sums[:8], axis=0)
    second = jnp.sum(sums[8:], axis=0)
    scores = first + jnp.concatenate([second[4:], second[:4]], axis=0) + probe_bias[...]
    scores_ref[...] = scores
    gated = scores / (1.0 + jnp.exp(-scores))
    logits_ref[...] = (
        jnp.dot(gated, head_weight[...], precision=lax.Precision.HIGHEST, preferred_element_type=jnp.float32)
        + head_bias[...]
    )


def finish(parts, probe_bias, head_weight, head_bias):
    rows, columns = parts.shape[1:]
    return pl.pallas_call(
        finish_kernel,
        out_shape=(
            jax.ShapeDtypeStruct((rows, columns), jnp.float32),
            jax.ShapeDtypeStruct((rows, head_weight.shape[1]), jnp.float32),
        ),
        in_specs=vmem(4),
        out_specs=tuple(vmem(2)),
        name="finish",
    )(parts, probe_bias.reshape(1, -1), head_weight, head_bias.reshape(1, -1))


def chip_body(
    queries,
    key_cache,
    value_cache,
    new_key,
    new_value,
    lengths,
    out_proj,
    residual,
    enc_weight,
    enc_bias,
    threshold_code,
    probe_weight,
    probe_bias,
    head_weight,
    head_bias,
):
    y, c = lax.axis_index("y"), lax.axis_index("c")
    width = out_proj.shape[1]
    proj_y = xor(out_proj, 16)
    enc_other = xor(enc_weight, 1)
    proj_c = xor(out_proj, 1)
    probe_other = xor(probe_weight, 1)
    levels = jnp.stack([enc_bias, threshold_code.astype(jnp.float32) / 16.0])
    levels_other = xor(levels, 1)
    bias = jnp.stack([levels[0], levels_other[0]])
    threshold = jnp.stack([levels[1], levels_other[1]])
    kept = residual.reshape(16, 2, 2, 4, width)
    kept_own = lax.dynamic_slice(kept, (0, c, y, 0, 0), (16, 1, 1, 4, width)).reshape(64, width)
    kept_given = lax.dynamic_slice(kept, (0, 1 - c, y, 0, 0), (16, 1, 1, 4, width)).reshape(64, width)
    kept_other = xor(kept_given, 1)
    proj_yc = xor(proj_y, 1)

    attended = attend(queries, key_cache, value_cache, new_key, new_value, lengths)
    half_width = attended.shape[1]
    split = attended.reshape(2, 2, 4, half_width).transpose(1, 0, 2, 3)
    sent = jnp.broadcast_to(split[:, None], (2, 8, 2, 4, half_width)).reshape(32, 4, half_width)
    taken = lax.all_to_all(sent, ALL, 0, 0, tiled=True).reshape(2, 64, half_width)
    mine = lax.dynamic_index_in_dim(taken, y, 0, keepdims=False)
    theirs = lax.dynamic_index_in_dim(taken, 1 - y, 0, keepdims=False)

    def project(kept_rows, near, far):
        projected = jnp.dot(mine, near, preferred_element_type=jnp.float32)
        projected = projected + jnp.dot(theirs, far, preferred_element_type=jnp.float32)
        return (kept_rows.astype(jnp.float32) + projected).astype(jnp.bfloat16)

    stream_own = project(kept_own, out_proj, proj_y)
    stream_other = project(kept_other, proj_c, proj_yc)
    stream = jnp.concatenate(
        [jnp.where(c == 0, stream_own, stream_other), jnp.where(c == 0, stream_other, stream_own)], axis=1
    )
    along_z = jnp.stack([stream, xor(stream, 4), xor(stream, 8), xor(stream, 12)])
    gathered = (along_z, xor(along_z, 2), xor(along_z, 16), xor(along_z, 18))
    partial = encode(gathered, (enc_weight, enc_other), bias, threshold, (probe_weight, probe_other))
    parts = lax.all_to_all(partial, PLANE, 0, 0, tiled=True)
    return finish(parts, probe_bias, head_weight, head_bias)


def body(
    queries,
    key_cache,
    value_cache,
    new_key,
    new_value,
    lengths,
    out_proj,
    residual,
    enc_weight,
    enc_bias,
    threshold_code,
    probe_weight,
    probe_bias,
    head_weight,
    head_bias,
):
    attended = attend(queries, key_cache, value_cache, new_key, new_value, lengths)
    partial_heads = jnp.dot(
        lax.all_gather(attended, "lat", axis=0, tiled=True),
        out_proj,
        preferred_element_type=jnp.float32,
    )
    projected = lax.psum(partial_heads, "tp")
    stream = (residual.astype(jnp.float32) + projected).astype(jnp.bfloat16)
    pre_act = jnp.dot(
        lax.all_gather(stream, "lat", axis=1, tiled=True),
        enc_weight,
        preferred_element_type=jnp.float32,
    )
    pre_act = pre_act + enc_bias
    threshold = threshold_code.astype(jnp.float32) / 16.0
    ramped = jnp.clip((pre_act - threshold) / RAMP_WIDTH, 0.0, 1.0)
    activations = (pre_act * ramped).astype(jnp.bfloat16)
    halfway = lax.psum_scatter(
        jnp.dot(activations, probe_weight, preferred_element_type=jnp.float32),
        "tp",
        scatter_dimension=0,
        tiled=True,
    )
    summed = lax.psum_scatter(halfway, "lat", scatter_dimension=0, tiled=True)
    probe_scores = summed + probe_bias
    harm_logits = (
        jnp.dot(
            jax.nn.silu(probe_scores),
            head_weight,
            precision=lax.Precision.HIGHEST,
            preferred_element_type=jnp.float32,
        )
        + head_bias
    )
    return (probe_scores, harm_logits)


def solution(mesh):
    chips = mesh.shape["tp"] == 2 and mesh.shape["lat"] == 16
    tp, lat = "tp", "lat"
    if chips:
        mesh = Mesh(mesh.devices.reshape(2, 4, 2, 2), ALL)
        tp, lat = ("y",), ("z", "x", "c")
    both = ALL if chips else ("tp", "lat")
    in_specs = (
        P(lat, tp),
        P(lat, None, tp),
        P(lat, None, tp),
        P(lat, tp),
        P(lat, tp),
        P(lat),
        P(tp, lat),
        P(None, lat),
        P(None, both),
        P(both),
        P(both),
        P(both, None),
        P(),
        P(),
        P(),
    )
    out_specs = (P(both, None), P(both, None))
    return jax.shard_map(
        chip_body if chips else body, mesh=mesh, in_specs=in_specs, out_specs=out_specs, check_vma=False
    )
```

```python
import jax
import jax.numpy as jnp
from jax import lax
from jax.experimental import pallas as pl
from jax.experimental.pallas import tpu as pltpu
from jax.sharding import Mesh, PartitionSpec as P

HEAD = 128


SOFT_CAP = 50.0
QUERY_SCALE = 1.0 / 12.0
RAMP_WIDTH = 0.25

ALL = ("y", "z", "x", "c")
PLANE = ("y", "z", "x")


def attend(queries, key_cache, value_cache, new_key, new_value, lengths):
    row_count, positions, kv_width = key_cache.shape
    kv_heads = kv_width // HEAD
    group_size = queries.shape[1] // kv_width
    grouped = queries.reshape(row_count, kv_heads, group_size, HEAD)
    key_rows = key_cache.reshape(row_count, positions, kv_heads, HEAD)
    values = value_cache.reshape(row_count, positions, kv_heads, HEAD)
    fresh_key = new_key.reshape(row_count, kv_heads, HEAD)
    fresh_value = new_value.reshape(row_count, kv_heads, 1, HEAD).astype(jnp.float32)
    cached = jnp.einsum("rkgd,rlkd->rkgl", grouped, key_rows, preferred_element_type=jnp.float32)
    own_score = jnp.einsum("rkgd,rkd->rkg", grouped, fresh_key, preferred_element_type=jnp.float32)
    cached = SOFT_CAP * jnp.tanh(cached * (QUERY_SCALE / SOFT_CAP))
    own_score = SOFT_CAP * jnp.tanh(own_score * (QUERY_SCALE / SOFT_CAP))
    live_mask = jnp.arange(positions, dtype=jnp.int32)[None, :] < lengths[:, None]
    cached_exp = jnp.where(live_mask[:, None, None, :], jnp.exp(cached), 0.0)
    own_exp = jnp.exp(own_score)
    denominator = jnp.sum(cached_exp, axis=-1) + own_exp
    cached_weight = (cached_exp / denominator[..., None]).astype(jnp.bfloat16)
    own_weight = (own_exp / denominator).astype(jnp.bfloat16)
    mixture = jnp.einsum(
        "rkgl,rlkd->rkgd", cached_weight, values, preferred_element_type=jnp.float32
    )
    mixture = mixture + own_weight.astype(jnp.float32)[..., None] * fresh_value
    return mixture.reshape(row_count, kv_heads * group_size * HEAD).astype(jnp.bfloat16)


def xor(value, bits):
    return lax.ppermute(value, ALL, [(i, i ^ bits) for i in range(32)])


def cost(seconds):
    return pl.CostEstimate(flops=0, bytes_accessed=int(seconds * 3.69e12), transcendentals=0)


def vmem(count):
    return [pl.BlockSpec(memory_space=pltpu.VMEM)] * count


def attend_kernel(
    lengths,
    queries,
    new_key,
    new_value,
    kept_own,
    kept_other,
    keys_at,
    values_at,
    out_ref,
    kept_ref,
    keys,
    values,
    heads,
    mixed,
    turned,
    arrived,
):
    row_count, positions, kv_width = keys.shape
    head_count = queries.shape[1] // HEAD
    kv_heads = kv_width // HEAD
    group = 4
    copies = []
    for at in range(row_count // group):
        rows = pl.ds(at * group, group)
        copies.append(pltpu.make_async_copy(keys_at.at[rows], keys.at[rows], arrived.at[0, at]))
        copies.append(pltpu.make_async_copy(values_at.at[rows], values.at[rows], arrived.at[1, at]))
    for copy in copies:
        copy.start()
    y, c = lax.axis_index("y"), lax.axis_index("c")
    for at, kept in enumerate((kept_own, kept_other)):
        turned[...] = kept[...].astype(jnp.float32).T
        for b in range(turned.shape[0] // 16):
            both = turned[pl.ds(pl.multiple_of(b * 16 + 8 * c, 8), 8), :]
            kept_ref[at, 4 * b : 4 * b + 4, :] = jnp.where(y == 0, both[:4], both[4:])
    for head in range(head_count):
        heads[pl.ds(head, row_count, stride=head_count), :] = queries[:, head * HEAD : (head + 1) * HEAD].astype(
            jnp.float32
        )
    shape = (head_count, kv_width)
    of_head = lax.broadcasted_iota(jnp.int32, shape, 0) // (head_count // kv_heads)
    in_block = of_head == lax.broadcasted_iota(jnp.int32, shape, 1) // HEAD
    place = lax.broadcasted_iota(jnp.int32, (head_count, positions), 1)
    fresh_key = new_key[...].astype(jnp.float32)
    fresh_value = new_value[...].astype(jnp.float32)

    def cap(score):
        return jnp.exp(SOFT_CAP * jnp.tanh(score * (QUERY_SCALE / SOFT_CAP)))

    for at in range(row_count // group):
        copies[2 * at].wait()
        weights, own_weights = [], []
        for row in range(at * group, (at + 1) * group):
            query = heads[row * head_count : (row + 1) * head_count, :]
            spread = jnp.where(in_block, jnp.concatenate([query] * kv_heads, axis=1), 0.0)
            scores = lax.dot_general(
                spread.astype(jnp.bfloat16),
                keys[row],
                (((1,), (1,)), ((), ())),
                preferred_element_type=jnp.float32,
            )
            own = cap(jnp.sum(spread * fresh_key[row : row + 1, :], axis=1, keepdims=True))
            exps = jnp.where(place < lengths[row], cap(scores), 0.0)
            scale = 1.0 / (jnp.sum(exps, axis=1, keepdims=True) + own)
            weights.append((exps * scale).astype(jnp.bfloat16))
            own_weights.append((own * scale).astype(jnp.bfloat16).astype(jnp.float32))
        copies[2 * at + 1].wait()
        for nth, row in enumerate(range(at * group, (at + 1) * group)):
            mixture = jnp.dot(weights[nth], values[row], preferred_element_type=jnp.float32)
            mixture = jnp.where(in_block, mixture + own_weights[nth] * fresh_value[row : row + 1, :], 0.0)
            folded = mixture[:, :HEAD]
            for kv_head in range(1, kv_heads):
                folded = folded + mixture[:, kv_head * HEAD : (kv_head + 1) * HEAD]
            heads[row * head_count : (row + 1) * head_count, :] = folded
    for head in range(head_count):
        mixed[:, head * HEAD : (head + 1) * HEAD] = heads[pl.ds(head, row_count, stride=head_count), :]
    for to_y in range(2):
        for to_c in range(2):
            share = mixed[8 * to_c + 4 * to_y : 8 * to_c + 4 * to_y + 4, :].astype(jnp.bfloat16)
            for zx in range(8):
                out_ref[to_y * 16 + zx * 2 + to_c] = share


def attend_shares(queries, key_cache, value_cache, new_key, new_value, lengths, kept_own, kept_other):
    rows, width = queries.shape
    features, row_count = kept_own.shape
    smem, hbm = pl.BlockSpec(memory_space=pltpu.SMEM), pl.BlockSpec(memory_space=pltpu.HBM)
    return pl.pallas_call(
        attend_kernel,
        out_shape=(
            jax.ShapeDtypeStruct((32, 4, width), jnp.bfloat16),
            jax.ShapeDtypeStruct((2, row_count // 4, features), jnp.float32),
        ),
        in_specs=[smem, *vmem(5), hbm, hbm],
        out_specs=tuple(vmem(2)),
        scratch_shapes=[
            pltpu.VMEM(key_cache.shape, key_cache.dtype),
            pltpu.VMEM(value_cache.shape, value_cache.dtype),
            pltpu.VMEM((rows * width // HEAD, HEAD), jnp.float32),
            pltpu.VMEM((rows, width), jnp.float32),
            pltpu.VMEM((row_count, features), jnp.float32),
            pltpu.SemaphoreType.DMA((2, rows // 4)),
        ],
        compiler_params=pltpu.CompilerParams(vmem_limit_bytes=56 * 1024 * 1024),
        cost_estimate=cost(12e-6),
        name="attend",
    )(lengths, queries, new_key, new_value, kept_own, kept_other, key_cache, value_cache)


ACROSS = (((1,), (1,)), ((), ()))


def after(value, other):
    def kernel(value_ref, other_ref, out_ref):
        pass

    anywhere = pl.BlockSpec(memory_space=pl.ANY)
    return pl.pallas_call(
        kernel,
        out_shape=jax.ShapeDtypeStruct(value.shape, value.dtype),
        in_specs=[anywhere] * 2,
        out_specs=anywhere,
        input_output_aliases={0: 0},
        compiler_params=pltpu.CompilerParams(vmem_limit_bytes=1024 * 1024),
        name="after",
    )(value, other)


def project_near_kernel(taken, weight_own, weight_other, kept, out_ref, far_ref, rows):
    y = lax.axis_index("y")
    blocks, share = taken.shape[0] // 2, taken.shape[1]
    for b in range(blocks):
        rows[0, b * share : (b + 1) * share, :] = taken[y * blocks + b].astype(jnp.float32)
        rows[1, b * share : (b + 1) * share, :] = taken[(1 - y) * blocks + b].astype(jnp.float32)
    far_ref[...] = rows[1].astype(jnp.bfloat16)
    near = rows[0].astype(jnp.bfloat16)
    for at, weight in enumerate((weight_own, weight_other)):
        out_ref[at] = kept[at] + lax.dot_general(near, weight[...], ACROSS, preferred_element_type=jnp.float32)


def project_far_kernel(far, weight_own, weight_other, near, out_ref):
    rows = far[...]
    own = near[0] + lax.dot_general(rows, weight_own[...], ACROSS, preferred_element_type=jnp.float32)
    other = near[1] + lax.dot_general(rows, weight_other[...], ACROSS, preferred_element_type=jnp.float32)
    core = lax.axis_index("c")
    first, second = jnp.where(core == 0, own, other), jnp.where(core == 0, other, own)
    stream = jnp.concatenate([first, second], axis=1).astype(jnp.bfloat16)
    half = stream.shape[0] // 2
    out_ref[0] = stream[:half]
    out_ref[1] = stream[half:]


def project_near(taken, weight_own, weight_other, kept):
    depth = taken.shape[2]
    rows = kept.shape[1]
    return pl.pallas_call(
        project_near_kernel,
        out_shape=(
            jax.ShapeDtypeStruct(kept.shape, jnp.float32),
            jax.ShapeDtypeStruct((rows, depth), taken.dtype),
        ),
        in_specs=vmem(4),
        out_specs=tuple(vmem(2)),
        scratch_shapes=[pltpu.VMEM((2, rows, depth), jnp.float32)],
        compiler_params=pltpu.CompilerParams(vmem_limit_bytes=16 * 1024 * 1024),
        cost_estimate=cost(2e-6),
        name="project_near",
    )(taken, weight_own, weight_other, kept)


def project_far(far, weight_own, weight_other, near):
    rows, width = near.shape[1:]
    return pl.pallas_call(
        project_far_kernel,
        out_shape=jax.ShapeDtypeStruct((2, rows // 2, 2 * width), jnp.bfloat16),
        in_specs=vmem(4),
        out_specs=pl.BlockSpec(memory_space=pltpu.VMEM),
        compiler_params=pltpu.CompilerParams(vmem_limit_bytes=16 * 1024 * 1024),
        cost_estimate=cost(2e-6),
        name="project_far",
    )(far, weight_own, weight_other, near)


def pre_activations(rows, weights):
    block = rows[0].shape[1]
    main = block // 256 * 256
    rest = jnp.concatenate([row[:, main:] for row in rows], axis=1)
    sums = []
    for half in range(2):
        total = None
        for dz, row in enumerate(rows):
            part = jnp.dot(row[:, :main], weights[half, dz, :main, :], preferred_element_type=jnp.float32)
            total = part if total is None else total + part
        ends = jnp.concatenate([weights[half, dz, main:, :] for dz in range(4)], axis=0)
        sums.append(total + jnp.dot(rest, ends, preferred_element_type=jnp.float32))
    return sums


def encode_first_kernel(own, other, enc_own, enc_other, out_ref, later_ref, weights, arrived):
    z, x = lax.axis_index("z"), lax.axis_index("x")
    block = own.shape[3]
    now, later = [], []
    for half, enc in enumerate((enc_own, enc_other)):
        for dz in range(4):
            for dx, to, copies in ((0, weights, now), (1, later_ref, later)):
                start = pl.multiple_of(((z ^ dz) * 2 + (x ^ dx)) * block, 64)
                sem = arrived.at[dx, half * 4 + dz]
                copies.append(pltpu.make_async_copy(enc.at[pl.ds(start, block)], to.at[half, dz], sem))
    for copy in now + later:
        copy.start()
    for copy in now:
        copy.wait()
    rows = [jnp.concatenate([own[0, dz], own[1, dz], other[0, dz], other[1, dz]], axis=0) for dz in range(4)]
    sums = pre_activations(rows, weights)
    out_ref[0] = sums[0]
    out_ref[1] = sums[1]
    for copy in later:
        copy.wait()


def encode_second_kernel(
    own, upper, lower, first, weights, bias, threshold, probe_own, probe_other, out_ref, ordered
):
    rows = [jnp.concatenate([own[0, dz], own[1, dz], upper[dz], lower[dz]], axis=0) for dz in range(4)]
    sums = pre_activations(rows, weights)
    partial = None
    for at, probe in enumerate((probe_own, probe_other)):
        pre = sums[at] + first[at] + bias[at : at + 1, :]
        ramped = jnp.clip((pre - threshold[at : at + 1, :]) / RAMP_WIDTH, 0.0, 1.0)
        active = (pre * ramped).astype(jnp.bfloat16)
        probed = jnp.dot(active, probe[...], preferred_element_type=jnp.float32)
        partial = probed if partial is None else partial + probed
    for half in range(2):
        for b in range(16):
            at = half * 64 + b * 4
            ordered[b, 4 * half : 4 * half + 4, :] = partial[at : at + 4, :]
    out_ref[...] = ordered[...].astype(jnp.bfloat16)


def encode_first(own, other, enc):
    rows, block, latents = 4 * own.shape[2], own.shape[3], enc[0].shape[1]
    weights = (2, 4, block, latents)
    hbm = pl.BlockSpec(memory_space=pltpu.HBM)
    return pl.pallas_call(
        encode_first_kernel,
        out_shape=(
            jax.ShapeDtypeStruct((2, rows, latents), jnp.float32),
            jax.ShapeDtypeStruct(weights, enc[0].dtype),
        ),
        in_specs=[*vmem(2), hbm, hbm],
        out_specs=tuple(vmem(2)),
        scratch_shapes=[pltpu.VMEM(weights, enc[0].dtype), pltpu.SemaphoreType.DMA((2, 8))],
        compiler_params=pltpu.CompilerParams(vmem_limit_bytes=48 * 1024 * 1024),
        cost_estimate=cost(2e-6),
        name="encode_first",
    )(own, other, *enc)


def encode_second(own, upper, lower, first, weights, bias, threshold, probe):
    columns = probe[0].shape[1]
    return pl.pallas_call(
        encode_second_kernel,
        out_shape=jax.ShapeDtypeStruct((16, 8, columns), jnp.bfloat16),
        in_specs=vmem(9),
        out_specs=pl.BlockSpec(memory_space=pltpu.VMEM),
        scratch_shapes=[pltpu.VMEM((16, 8, columns), jnp.float32)],
        compiler_params=pltpu.CompilerParams(vmem_limit_bytes=24 * 1024 * 1024),
        cost_estimate=cost(2e-6),
        name="encode_second",
    )(own, upper, lower, first, weights, bias, threshold, *probe)


def finish_kernel(parts, probe_bias, head_weight, head_bias, scores_ref, logits_ref):
    sums = parts[...].astype(jnp.float32)
    first = jnp.sum(sums[:8], axis=0)
    second = jnp.sum(sums[8:], axis=0)
    scores = first + jnp.concatenate([second[4:], second[:4]], axis=0) + probe_bias[...]
    scores_ref[...] = scores
    gated = scores / (1.0 + jnp.exp(-scores))
    logits_ref[...] = (
        lax.dot_general(
            gated,
            head_weight[...],
            (((1,), (1,)), ((), ())),
            precision=lax.Precision.HIGHEST,
            preferred_element_type=jnp.float32,
        )
        + head_bias[...]
    )


def finish(parts, probe_bias, head_weight, head_bias):
    rows, columns = parts.shape[1:]
    return pl.pallas_call(
        finish_kernel,
        out_shape=(
            jax.ShapeDtypeStruct((rows, columns), jnp.float32),
            jax.ShapeDtypeStruct((rows, head_weight.shape[1]), jnp.float32),
        ),
        in_specs=vmem(4),
        out_specs=tuple(vmem(2)),
        compiler_params=pltpu.CompilerParams(vmem_limit_bytes=8 * 1024 * 1024),
        name="finish",
    )(parts, probe_bias.reshape(1, -1), head_weight.T, head_bias.reshape(1, -1))


def chip_body(
    queries,
    key_cache,
    value_cache,
    new_key,
    new_value,
    lengths,
    out_proj,
    residual,
    enc_weight,
    enc_bias,
    threshold_code,
    probe_weight,
    probe_bias,
    head_weight,
    head_bias,
):
    proj = out_proj.T
    proj_y = xor(proj, 16)
    enc_other = xor(enc_weight, 1)
    proj_c = xor(proj, 1)
    probe_other = xor(probe_weight, 1)
    levels = jnp.stack([enc_bias, threshold_code.astype(jnp.float32) / 16.0])
    levels_other = xor(levels, 1)
    bias = jnp.stack([levels[0], levels_other[0]])
    threshold = jnp.stack([levels[1], levels_other[1]])
    kept = residual.T
    kept_other = xor(kept, 1)

    sent, kept_rows = attend_shares(
        queries, key_cache, value_cache, new_key, new_value, lengths, kept, kept_other
    )
    taken = lax.all_to_all(sent, ALL, 0, 0, tiled=True)
    proj_y = after(proj_y, taken)
    proj_yc = xor(proj_y, 1)
    near, far = project_near(taken, proj, proj_c, kept_rows)
    stream = project_far(far, proj_y, proj_yc, near)
    along_z = jnp.stack([stream, xor(stream, 4), xor(stream, 8), xor(stream, 12)], axis=1)
    over_y, over_x = xor(along_z, 16), xor(along_z, 2)
    upper, lower = xor(over_x[0], 16), xor(over_y[1], 2)
    first, weights = encode_first(along_z, over_y, (enc_weight, enc_other))
    partial = encode_second(
        over_x, upper, lower, first, weights, bias, threshold, (probe_weight, probe_other)
    )
    parts = lax.all_to_all(partial, PLANE, 0, 0, tiled=True)
    return finish(parts, probe_bias, head_weight, head_bias)


def body(
    queries,
    key_cache,
    value_cache,
    new_key,
    new_value,
    lengths,
    out_proj,
    residual,
    enc_weight,
    enc_bias,
    threshold_code,
    probe_weight,
    probe_bias,
    head_weight,
    head_bias,
):
    attended = attend(queries, key_cache, value_cache, new_key, new_value, lengths)
    partial_heads = jnp.dot(
        lax.all_gather(attended, "lat", axis=0, tiled=True),
        out_proj,
        preferred_element_type=jnp.float32,
    )
    projected = lax.psum(partial_heads, "tp")
    stream = (residual.astype(jnp.float32) + projected).astype(jnp.bfloat16)
    pre_act = jnp.dot(
        lax.all_gather(stream, "lat", axis=1, tiled=True),
        enc_weight,
        preferred_element_type=jnp.float32,
    )
    pre_act = pre_act + enc_bias
    threshold = threshold_code.astype(jnp.float32) / 16.0
    ramped = jnp.clip((pre_act - threshold) / RAMP_WIDTH, 0.0, 1.0)
    activations = (pre_act * ramped).astype(jnp.bfloat16)
    halfway = lax.psum_scatter(
        jnp.dot(activations, probe_weight, preferred_element_type=jnp.float32),
        "tp",
        scatter_dimension=0,
        tiled=True,
    )
    summed = lax.psum_scatter(halfway, "lat", scatter_dimension=0, tiled=True)
    probe_scores = summed + probe_bias
    harm_logits = (
        jnp.dot(
            jax.nn.silu(probe_scores),
            head_weight,
            precision=lax.Precision.HIGHEST,
            preferred_element_type=jnp.float32,
        )
        + head_bias
    )
    return (probe_scores, harm_logits)


def solution(mesh):
    chips = mesh.shape["tp"] == 2 and mesh.shape["lat"] == 16
    tp, lat = "tp", "lat"
    if chips:
        mesh = Mesh(mesh.devices.reshape(2, 4, 2, 2), ALL)
        tp, lat = ("y",), ("z", "x", "c")
    both = ALL if chips else ("tp", "lat")
    in_specs = (
        P(lat, tp),
        P(lat, None, tp),
        P(lat, None, tp),
        P(lat, tp),
        P(lat, tp),
        P(lat),
        P(tp, lat),
        P(None, lat),
        P(None, both),
        P(both),
        P(both),
        P(both, None),
        P(),
        P(),
        P(),
    )
    out_specs = (P(both, None), P(both, None))
    return jax.shard_map(
        chip_body if chips else body, mesh=mesh, in_specs=in_specs, out_specs=out_specs, check_vma=False
    )
```

```python
import jax
import jax.numpy as jnp
from jax import lax
from jax.experimental import pallas as pl
from jax.experimental.pallas import tpu as pltpu
from jax.sharding import Mesh, PartitionSpec as P

HEAD = 128


SOFT_CAP = 50.0
QUERY_SCALE = 1.0 / 12.0
RAMP_WIDTH = 0.25

ALL = ("y", "z", "x", "c")
PLANE = ("y", "z", "x")


def attend(queries, key_cache, value_cache, new_key, new_value, lengths):
    row_count, positions, kv_width = key_cache.shape
    kv_heads = kv_width // HEAD
    group_size = queries.shape[1] // kv_width
    grouped = queries.reshape(row_count, kv_heads, group_size, HEAD)
    key_rows = key_cache.reshape(row_count, positions, kv_heads, HEAD)
    values = value_cache.reshape(row_count, positions, kv_heads, HEAD)
    fresh_key = new_key.reshape(row_count, kv_heads, HEAD)
    fresh_value = new_value.reshape(row_count, kv_heads, 1, HEAD).astype(jnp.float32)
    cached = jnp.einsum("rkgd,rlkd->rkgl", grouped, key_rows, preferred_element_type=jnp.float32)
    own_score = jnp.einsum("rkgd,rkd->rkg", grouped, fresh_key, preferred_element_type=jnp.float32)
    cached = SOFT_CAP * jnp.tanh(cached * (QUERY_SCALE / SOFT_CAP))
    own_score = SOFT_CAP * jnp.tanh(own_score * (QUERY_SCALE / SOFT_CAP))
    live_mask = jnp.arange(positions, dtype=jnp.int32)[None, :] < lengths[:, None]
    cached_exp = jnp.where(live_mask[:, None, None, :], jnp.exp(cached), 0.0)
    own_exp = jnp.exp(own_score)
    denominator = jnp.sum(cached_exp, axis=-1) + own_exp
    cached_weight = (cached_exp / denominator[..., None]).astype(jnp.bfloat16)
    own_weight = (own_exp / denominator).astype(jnp.bfloat16)
    mixture = jnp.einsum(
        "rkgl,rlkd->rkgd", cached_weight, values, preferred_element_type=jnp.float32
    )
    mixture = mixture + own_weight.astype(jnp.float32)[..., None] * fresh_value
    return mixture.reshape(row_count, kv_heads * group_size * HEAD).astype(jnp.bfloat16)


def xor(value, bits):
    return lax.ppermute(value, ALL, [(i, i ^ bits) for i in range(32)])


def cost(seconds):
    return pl.CostEstimate(flops=0, bytes_accessed=int(seconds * 3.69e12), transcendentals=0)


def vmem(count):
    return [pl.BlockSpec(memory_space=pltpu.VMEM)] * count


def attend_kernel(
    lengths,
    queries,
    new_key,
    new_value,
    keys_at,
    values_at,
    out_ref,
    keys,
    values,
    heads,
    mixed,
    arrived,
):
    row_count, positions, kv_width = keys.shape
    head_count = queries.shape[1] // HEAD
    kv_heads = kv_width // HEAD
    group = 4
    copies = []
    for at in range(row_count // group):
        rows = pl.ds(at * group, group)
        copies.append(pltpu.make_async_copy(keys_at.at[rows], keys.at[rows], arrived.at[0, at]))
        copies.append(pltpu.make_async_copy(values_at.at[rows], values.at[rows], arrived.at[1, at]))
    for copy in copies:
        copy.start()
    for head in range(head_count):
        heads[pl.ds(head, row_count, stride=head_count), :] = queries[:, head * HEAD : (head + 1) * HEAD].astype(
            jnp.float32
        )
    shape = (head_count, kv_width)
    of_head = lax.broadcasted_iota(jnp.int32, shape, 0) // (head_count // kv_heads)
    in_block = of_head == lax.broadcasted_iota(jnp.int32, shape, 1) // HEAD
    place = lax.broadcasted_iota(jnp.int32, (head_count, positions), 1)
    fresh_key = new_key[...].astype(jnp.float32)
    fresh_value = new_value[...].astype(jnp.float32)

    def cap(score):
        return jnp.exp(SOFT_CAP * jnp.tanh(score * (QUERY_SCALE / SOFT_CAP)))

    for at in range(row_count // group):
        copies[2 * at].wait()
        weights, own_weights = [], []
        for row in range(at * group, (at + 1) * group):
            query = heads[row * head_count : (row + 1) * head_count, :]
            spread = jnp.where(in_block, jnp.concatenate([query] * kv_heads, axis=1), 0.0)
            scores = lax.dot_general(
                spread.astype(jnp.bfloat16),
                keys[row],
                (((1,), (1,)), ((), ())),
                preferred_element_type=jnp.float32,
            )
            own = cap(jnp.sum(spread * fresh_key[row : row + 1, :], axis=1, keepdims=True))
            exps = jnp.where(place < lengths[row], cap(scores), 0.0)
            scale = 1.0 / (jnp.sum(exps, axis=1, keepdims=True) + own)
            weights.append((exps * scale).astype(jnp.bfloat16))
            own_weights.append((own * scale).astype(jnp.bfloat16).astype(jnp.float32))
        copies[2 * at + 1].wait()
        for nth, row in enumerate(range(at * group, (at + 1) * group)):
            mixture = jnp.dot(weights[nth], values[row], preferred_element_type=jnp.float32)
            mixture = jnp.where(in_block, mixture + own_weights[nth] * fresh_value[row : row + 1, :], 0.0)
            folded = mixture[:, :HEAD]
            for kv_head in range(1, kv_heads):
                folded = folded + mixture[:, kv_head * HEAD : (kv_head + 1) * HEAD]
            heads[row * head_count : (row + 1) * head_count, :] = folded
    for head in range(head_count):
        mixed[:, head * HEAD : (head + 1) * HEAD] = heads[pl.ds(head, row_count, stride=head_count), :]
    for to_y in range(2):
        for to_c in range(2):
            share = mixed[8 * to_c + 4 * to_y : 8 * to_c + 4 * to_y + 4, :].astype(jnp.bfloat16)
            for zx in range(8):
                out_ref[to_y * 16 + zx * 2 + to_c] = share


def attend_shares(queries, key_cache, value_cache, new_key, new_value, lengths):
    rows, width = queries.shape
    smem, hbm = pl.BlockSpec(memory_space=pltpu.SMEM), pl.BlockSpec(memory_space=pltpu.HBM)
    return pl.pallas_call(
        attend_kernel,
        out_shape=jax.ShapeDtypeStruct((32, 4, width), jnp.bfloat16),
        in_specs=[smem, *vmem(3), hbm, hbm],
        out_specs=pl.BlockSpec(memory_space=pltpu.VMEM),
        scratch_shapes=[
            pltpu.VMEM(key_cache.shape, key_cache.dtype),
            pltpu.VMEM(value_cache.shape, value_cache.dtype),
            pltpu.VMEM((rows * width // HEAD, HEAD), jnp.float32),
            pltpu.VMEM((rows, width), jnp.float32),
            pltpu.SemaphoreType.DMA((2, rows // 4)),
        ],
        compiler_params=pltpu.CompilerParams(vmem_limit_bytes=56 * 1024 * 1024),
        cost_estimate=cost(12e-6),
        name="attend",
    )(lengths, queries, new_key, new_value, key_cache, value_cache)


ACROSS = (((1,), (1,)), ((), ()))


def keep_kernel(kept_own, kept_other, *rest):
    out_ref, token_ref, turned = rest[-3:]
    token_ref[...] = jnp.zeros_like(token_ref)
    y, c = lax.axis_index("y"), lax.axis_index("c")
    for at, kept in enumerate((kept_own, kept_other)):
        turned[...] = kept[...].astype(jnp.float32).T
        for b in range(turned.shape[0] // 16):
            both = turned[pl.ds(pl.multiple_of(b * 16 + 8 * c, 8), 8), :]
            out_ref[at, 4 * b : 4 * b + 4, :] = jnp.where(y == 0, both[:4], both[4:])


def keep(kept_own, kept_other, ready):
    features, rows = kept_own.shape
    return pl.pallas_call(
        keep_kernel,
        out_shape=(
            jax.ShapeDtypeStruct((2, rows // 4, features), jnp.float32),
            jax.ShapeDtypeStruct((8, 128), jnp.float32),
        ),
        in_specs=vmem(2) + [pl.BlockSpec(memory_space=pl.ANY)] * len(ready),
        out_specs=tuple(vmem(2)),
        scratch_shapes=[pltpu.VMEM((rows, features), jnp.float32)],
        compiler_params=pltpu.CompilerParams(vmem_limit_bytes=4 * 1024 * 1024),
        cost_estimate=cost(1e-6),
        name="keep",
    )(kept_own, kept_other, *ready)


def after(value, other, limit=1024 * 1024):
    def kernel(value_ref, other_ref, out_ref):
        pass

    anywhere = pl.BlockSpec(memory_space=pl.ANY)
    return pl.pallas_call(
        kernel,
        out_shape=jax.ShapeDtypeStruct(value.shape, value.dtype),
        in_specs=[anywhere] * 2,
        out_specs=anywhere,
        input_output_aliases={0: 0},
        compiler_params=pltpu.CompilerParams(vmem_limit_bytes=limit),
        name="after",
    )(value, other)


def project_near_kernel(taken, weight_own, weight_other, kept, out_ref, far_ref, rows):
    y = lax.axis_index("y")
    blocks, share = taken.shape[0] // 2, taken.shape[1]
    for b in range(blocks):
        rows[0, b * share : (b + 1) * share, :] = taken[y * blocks + b].astype(jnp.float32)
        rows[1, b * share : (b + 1) * share, :] = taken[(1 - y) * blocks + b].astype(jnp.float32)
    far_ref[...] = rows[1].astype(jnp.bfloat16)
    near = rows[0].astype(jnp.bfloat16)
    for at, weight in enumerate((weight_own, weight_other)):
        out_ref[at] = kept[at] + lax.dot_general(near, weight[...], ACROSS, preferred_element_type=jnp.float32)


def project_far_kernel(far, weight_own, weight_other, near, out_ref):
    rows = far[...]
    own = near[0] + lax.dot_general(rows, weight_own[...], ACROSS, preferred_element_type=jnp.float32)
    other = near[1] + lax.dot_general(rows, weight_other[...], ACROSS, preferred_element_type=jnp.float32)
    core = lax.axis_index("c")
    first, second = jnp.where(core == 0, own, other), jnp.where(core == 0, other, own)
    stream = jnp.concatenate([first, second], axis=1).astype(jnp.bfloat16)
    half = stream.shape[0] // 2
    out_ref[0] = stream[:half]
    out_ref[1] = stream[half:]


def project_near(taken, weight_own, weight_other, kept):
    depth = taken.shape[2]
    rows = kept.shape[1]
    return pl.pallas_call(
        project_near_kernel,
        out_shape=(
            jax.ShapeDtypeStruct(kept.shape, jnp.float32),
            jax.ShapeDtypeStruct((rows, depth), taken.dtype),
        ),
        in_specs=vmem(4),
        out_specs=tuple(vmem(2)),
        scratch_shapes=[pltpu.VMEM((2, rows, depth), jnp.float32)],
        compiler_params=pltpu.CompilerParams(vmem_limit_bytes=16 * 1024 * 1024),
        cost_estimate=cost(2e-6),
        name="project_near",
    )(taken, weight_own, weight_other, kept)


def project_far(far, weight_own, weight_other, near):
    rows, width = near.shape[1:]
    return pl.pallas_call(
        project_far_kernel,
        out_shape=jax.ShapeDtypeStruct((2, rows // 2, 2 * width), jnp.bfloat16),
        in_specs=vmem(4),
        out_specs=pl.BlockSpec(memory_space=pltpu.VMEM),
        compiler_params=pltpu.CompilerParams(vmem_limit_bytes=16 * 1024 * 1024),
        cost_estimate=cost(2e-6),
        name="project_far",
    )(far, weight_own, weight_other, near)


def pre_activations(rows, weights):
    block = rows[0].shape[1]
    main = block // 256 * 256
    rest = jnp.concatenate([row[:, main:] for row in rows], axis=1)
    sums = []
    for half in range(2):
        total = None
        for dz, row in enumerate(rows):
            part = jnp.dot(row[:, :main], weights[half, dz, :main, :], preferred_element_type=jnp.float32)
            total = part if total is None else total + part
        ends = jnp.concatenate([weights[half, dz, main:, :] for dz in range(4)], axis=0)
        sums.append(total + jnp.dot(rest, ends, preferred_element_type=jnp.float32))
    return sums


def encode_first_kernel(own, other, own_far, other_far, enc_own, enc_other, out_ref, later_ref, weights, arrived):
    z, x = lax.axis_index("z"), lax.axis_index("x")
    block = own.shape[3]
    pairs = ((own, other), (own_far, other_far))
    now, later = [], []
    for half, enc in enumerate((enc_own, enc_other)):
        for dz in range(4):
            for dx, to, copies in ((0, weights, now), (1, later_ref, later)):
                start = pl.multiple_of(((z ^ dz) * 2 + (x ^ dx)) * block, 64)
                sem = arrived.at[dx, half * 4 + dz]
                copies.append(pltpu.make_async_copy(enc.at[pl.ds(start, block)], to.at[half, dz], sem))
    for copy in now + later:
        copy.start()
    for copy in now:
        copy.wait()
    rows = [
        jnp.concatenate([piece[half, dz] for piece in pair for half in range(2)], axis=0)
        for pair in pairs
        for dz in range(2)
    ]
    sums = pre_activations(rows, weights)
    out_ref[0] = sums[0]
    out_ref[1] = sums[1]
    for copy in later:
        copy.wait()


def encode_second_kernel(
    own,
    upper,
    lower,
    own_far,
    upper_far,
    lower_far,
    first,
    weights,
    bias_own,
    code_own,
    probe_own,
    bias_other,
    code_other,
    probe_other,
    out_ref,
    ordered,
):
    rows = [
        jnp.concatenate([piece[0, dz], piece[1, dz], up[dz], low[dz]], axis=0)
        for piece, up, low in ((own, upper, lower), (own_far, upper_far, lower_far))
        for dz in range(2)
    ]
    sums = pre_activations(rows, weights)
    partial = None
    halves = ((bias_own, code_own, probe_own), (bias_other, code_other, probe_other))
    for at, (bias, code, probe) in enumerate(halves):
        pre = sums[at] + first[at] + bias[...]
        threshold = code[...].astype(jnp.float32) / 16.0
        ramped = jnp.clip((pre - threshold) / RAMP_WIDTH, 0.0, 1.0)
        active = (pre * ramped).astype(jnp.bfloat16)
        probed = jnp.dot(active, probe[...], preferred_element_type=jnp.float32)
        partial = probed if partial is None else partial + probed
    for half in range(2):
        for b in range(16):
            at = half * 64 + b * 4
            ordered[b, 4 * half : 4 * half + 4, :] = partial[at : at + 4, :]
    out_ref[...] = ordered[...].astype(jnp.bfloat16)


def encode_first(near, far, enc):
    own = near[0]
    rows, block, latents = 4 * own.shape[2], own.shape[3], enc[0].shape[1]
    weights = (2, 4, block, latents)
    hbm = pl.BlockSpec(memory_space=pltpu.HBM)
    return pl.pallas_call(
        encode_first_kernel,
        out_shape=(
            jax.ShapeDtypeStruct((2, rows, latents), jnp.float32),
            jax.ShapeDtypeStruct(weights, enc[0].dtype),
        ),
        in_specs=[*vmem(4), hbm, hbm],
        out_specs=tuple(vmem(2)),
        scratch_shapes=[pltpu.VMEM(weights, enc[0].dtype), pltpu.SemaphoreType.DMA((2, 8))],
        compiler_params=pltpu.CompilerParams(vmem_limit_bytes=50 * 1024 * 1024),
        cost_estimate=cost(2e-6),
        name="encode_first",
    )(*near, *far, *enc)


def encode_second(near, far, first, weights, own, other):
    columns = own[2].shape[1]
    return pl.pallas_call(
        encode_second_kernel,
        out_shape=jax.ShapeDtypeStruct((16, 8, columns), jnp.bfloat16),
        in_specs=vmem(14),
        out_specs=pl.BlockSpec(memory_space=pltpu.VMEM),
        scratch_shapes=[pltpu.VMEM((16, 8, columns), jnp.float32)],
        compiler_params=pltpu.CompilerParams(vmem_limit_bytes=24 * 1024 * 1024),
        cost_estimate=cost(2e-6),
        name="encode_second",
    )(*near, *far, first, weights, *own, *other)


def finish_kernel(parts, probe_bias, head_weight, head_bias, scores_ref, logits_ref):
    sums = parts[...].astype(jnp.float32)
    first = jnp.sum(sums[:8], axis=0)
    second = jnp.sum(sums[8:], axis=0)
    scores = first + jnp.concatenate([second[4:], second[:4]], axis=0) + probe_bias[...]
    scores_ref[...] = scores
    gated = scores / (1.0 + jnp.exp(-scores))
    logits_ref[...] = (
        lax.dot_general(
            gated,
            head_weight[...],
            (((1,), (1,)), ((), ())),
            precision=lax.Precision.HIGHEST,
            preferred_element_type=jnp.float32,
        )
        + head_bias[...]
    )


def finish(parts, probe_bias, head_weight, head_bias):
    rows, columns = parts.shape[1:]
    return pl.pallas_call(
        finish_kernel,
        out_shape=(
            jax.ShapeDtypeStruct((rows, columns), jnp.float32),
            jax.ShapeDtypeStruct((rows, head_weight.shape[1]), jnp.float32),
        ),
        in_specs=vmem(4),
        out_specs=tuple(vmem(2)),
        compiler_params=pltpu.CompilerParams(vmem_limit_bytes=8 * 1024 * 1024),
        name="finish",
    )(parts, probe_bias.reshape(1, -1), head_weight.T, head_bias.reshape(1, -1))


def chip_body(
    queries,
    key_cache,
    value_cache,
    new_key,
    new_value,
    lengths,
    out_proj,
    residual,
    enc_weight,
    enc_bias,
    threshold_code,
    probe_weight,
    probe_bias,
    head_weight,
    head_bias,
):
    proj = out_proj.T
    proj_y = xor(proj, 16)
    enc_other = xor(enc_weight, 1)
    proj_c = xor(proj, 1)
    probe_other = xor(probe_weight, 1)
    bias_other, code_other = xor(enc_bias, 1), xor(threshold_code, 1)
    kept = residual.T
    kept_other = xor(kept, 1)

    sent = attend_shares(queries, key_cache, value_cache, new_key, new_value, lengths)
    kept_rows, token = keep(kept, kept_other, (probe_other, bias_other, code_other))
    sent = after(sent, token, 56 * 1024 * 1024)
    taken = lax.all_to_all(sent, ALL, 0, 0, tiled=True)
    proj_y = after(proj_y, taken)
    proj_yc = xor(proj_y, 1)
    near, far = project_near(taken, proj, proj_c, kept_rows)
    stream = project_far(far, proj_y, proj_yc, near)
    along_z = [stream, xor(stream, 4), xor(stream, 8), xor(stream, 12)]

    def spread(mine):
        over_y, over_x = xor(mine, 16), xor(mine, 2)
        return (mine, over_y), (over_x, xor(over_x[0], 16), xor(over_y[1], 2))

    first_near, second_near = spread(jnp.stack(along_z[:2], axis=1))
    first_far, second_far = spread(after(jnp.stack(along_z[2:], axis=1), second_near[0]))
    first, weights = encode_first(first_near, first_far, (enc_weight, enc_other))
    partial = encode_second(
        second_near,
        second_far,
        first,
        weights,
        (enc_bias[None], threshold_code[None], probe_weight),
        (bias_other[None], code_other[None], probe_other),
    )
    parts = lax.all_to_all(partial, PLANE, 0, 0, tiled=True)
    return finish(parts, probe_bias, head_weight, head_bias)


def body(
    queries,
    key_cache,
    value_cache,
    new_key,
    new_value,
    lengths,
    out_proj,
    residual,
    enc_weight,
    enc_bias,
    threshold_code,
    probe_weight,
    probe_bias,
    head_weight,
    head_bias,
):
    attended = attend(queries, key_cache, value_cache, new_key, new_value, lengths)
    partial_heads = jnp.dot(
        lax.all_gather(attended, "lat", axis=0, tiled=True),
        out_proj,
        preferred_element_type=jnp.float32,
    )
    projected = lax.psum(partial_heads, "tp")
    stream = (residual.astype(jnp.float32) + projected).astype(jnp.bfloat16)
    pre_act = jnp.dot(
        lax.all_gather(stream, "lat", axis=1, tiled=True),
        enc_weight,
        preferred_element_type=jnp.float32,
    )
    pre_act = pre_act + enc_bias
    threshold = threshold_code.astype(jnp.float32) / 16.0
    ramped = jnp.clip((pre_act - threshold) / RAMP_WIDTH, 0.0, 1.0)
    activations = (pre_act * ramped).astype(jnp.bfloat16)
    halfway = lax.psum_scatter(
        jnp.dot(activations, probe_weight, preferred_element_type=jnp.float32),
        "tp",
        scatter_dimension=0,
        tiled=True,
    )
    summed = lax.psum_scatter(halfway, "lat", scatter_dimension=0, tiled=True)
    probe_scores = summed + probe_bias
    harm_logits = (
        jnp.dot(
            jax.nn.silu(probe_scores),
            head_weight,
            precision=lax.Precision.HIGHEST,
            preferred_element_type=jnp.float32,
        )
        + head_bias
    )
    return (probe_scores, harm_logits)


def solution(mesh):
    chips = mesh.shape["tp"] == 2 and mesh.shape["lat"] == 16
    tp, lat = "tp", "lat"
    if chips:
        mesh = Mesh(mesh.devices.reshape(2, 4, 2, 2), ALL)
        tp, lat = ("y",), ("z", "x", "c")
    both = ALL if chips else ("tp", "lat")
    in_specs = (
        P(lat, tp),
        P(lat, None, tp),
        P(lat, None, tp),
        P(lat, tp),
        P(lat, tp),
        P(lat),
        P(tp, lat),
        P(None, lat),
        P(None, both),
        P(both),
        P(both),
        P(both, None),
        P(),
        P(),
        P(),
    )
    out_specs = (P(both, None), P(both, None))
    return jax.shard_map(
        chip_body if chips else body, mesh=mesh, in_specs=in_specs, out_specs=out_specs, check_vma=False
    )
```

```python
import jax
import jax.numpy as jnp
from jax import lax
from jax.experimental import pallas as pl
from jax.experimental.pallas import tpu as pltpu
from jax.sharding import Mesh, PartitionSpec as P

HEAD = 128


SOFT_CAP = 50.0
QUERY_SCALE = 1.0 / 12.0
RAMP_WIDTH = 0.25
ACROSS = (((1,), (1,)), ((), ()))

ALL = ("y", "z", "x", "c")
PLANE = ("y", "z", "x")


def attend(queries, key_cache, value_cache, new_key, new_value, lengths):
    row_count, positions, kv_width = key_cache.shape
    kv_heads = kv_width // HEAD
    group_size = queries.shape[1] // kv_width
    grouped = queries.reshape(row_count, kv_heads, group_size, HEAD)
    key_rows = key_cache.reshape(row_count, positions, kv_heads, HEAD)
    values = value_cache.reshape(row_count, positions, kv_heads, HEAD)
    fresh_key = new_key.reshape(row_count, kv_heads, HEAD)
    fresh_value = new_value.reshape(row_count, kv_heads, 1, HEAD).astype(jnp.float32)
    cached = jnp.einsum("rkgd,rlkd->rkgl", grouped, key_rows, preferred_element_type=jnp.float32)
    own_score = jnp.einsum("rkgd,rkd->rkg", grouped, fresh_key, preferred_element_type=jnp.float32)
    cached = SOFT_CAP * jnp.tanh(cached * (QUERY_SCALE / SOFT_CAP))
    own_score = SOFT_CAP * jnp.tanh(own_score * (QUERY_SCALE / SOFT_CAP))
    live_mask = jnp.arange(positions, dtype=jnp.int32)[None, :] < lengths[:, None]
    cached_exp = jnp.where(live_mask[:, None, None, :], jnp.exp(cached), 0.0)
    own_exp = jnp.exp(own_score)
    denominator = jnp.sum(cached_exp, axis=-1) + own_exp
    cached_weight = (cached_exp / denominator[..., None]).astype(jnp.bfloat16)
    own_weight = (own_exp / denominator).astype(jnp.bfloat16)
    mixture = jnp.einsum(
        "rkgl,rlkd->rkgd", cached_weight, values, preferred_element_type=jnp.float32
    )
    mixture = mixture + own_weight.astype(jnp.float32)[..., None] * fresh_value
    return mixture.reshape(row_count, kv_heads * group_size * HEAD).astype(jnp.bfloat16)


def xor(value, bits):
    return lax.ppermute(value, ALL, [(i, i ^ bits) for i in range(32)])


def cost(seconds):
    return pl.CostEstimate(flops=0, bytes_accessed=int(seconds * 3.69e12), transcendentals=0)


def vmem(count):
    return [pl.BlockSpec(memory_space=pltpu.VMEM)] * count


def attend_kernel(
    lengths,
    queries,
    new_key,
    new_value,
    keys_at,
    values_at,
    out_ref,
    keys,
    values,
    heads,
    mixed,
    arrived,
):
    row_count, positions, kv_width = keys.shape
    head_count = queries.shape[1] // HEAD
    kv_heads = kv_width // HEAD
    group = 4
    groups = [range(at, at + group) for at in range(0, row_count, group)]
    copies = []
    for at in range(len(groups)):
        rows = pl.ds(at * group, group)
        copies.append(
            (
                pltpu.make_async_copy(keys_at.at[rows], keys.at[rows], arrived.at[0, at]),
                pltpu.make_async_copy(values_at.at[rows], values.at[rows], arrived.at[1, at]),
            )
        )
    copies[0][0].start()
    for at in range(len(groups)):
        if at + 1 < len(groups):
            copies[at + 1][0].start()
        copies[at][1].start()
    for head in range(head_count):
        heads[pl.ds(head, row_count, stride=head_count), :] = queries[:, head * HEAD : (head + 1) * HEAD].astype(
            jnp.float32
        )
    shape = (head_count, kv_width)
    of_head = lax.broadcasted_iota(jnp.int32, shape, 0) // (head_count // kv_heads)
    in_block = of_head == lax.broadcasted_iota(jnp.int32, shape, 1) // HEAD
    place = lax.broadcasted_iota(jnp.int32, (head_count, positions), 1)
    fresh_key = new_key[...].astype(jnp.float32)
    fresh_value = new_value[...].astype(jnp.float32)

    def cap(score):
        return jnp.exp(SOFT_CAP * jnp.tanh(score * (QUERY_SCALE / SOFT_CAP)))

    def weigh(row):
        query = heads[row * head_count : (row + 1) * head_count, :]
        spread = jnp.where(in_block, jnp.concatenate([query] * kv_heads, axis=1), 0.0)
        scores = lax.dot_general(
            spread.astype(jnp.bfloat16), keys[row], ACROSS, preferred_element_type=jnp.float32
        )
        own = cap(jnp.sum(spread * fresh_key[row : row + 1, :], axis=1, keepdims=True))
        exps = jnp.where(place < lengths[row], cap(scores), 0.0)
        scale = 1.0 / (jnp.sum(exps, axis=1, keepdims=True) + own)
        return (exps * scale).astype(jnp.bfloat16), (own * scale).astype(jnp.bfloat16).astype(jnp.float32)

    def mix(row, weights, own_weight):
        mixture = jnp.dot(weights, values[row], preferred_element_type=jnp.float32)
        mixture = jnp.where(in_block, mixture + own_weight * fresh_value[row : row + 1, :], 0.0)
        folded = mixture[:, :HEAD]
        for kv_head in range(1, kv_heads):
            folded = folded + mixture[:, kv_head * HEAD : (kv_head + 1) * HEAD]
        return folded

    copies[0][0].wait()
    weighed = [weigh(row) for row in groups[0]]
    for at in range(len(groups)):
        copies[at][1].wait()
        if at + 1 < len(groups):
            copies[at + 1][0].wait()
            following = [weigh(row) for row in groups[at + 1]]
        folded = [mix(row, *weighed[nth]) for nth, row in enumerate(groups[at])]
        mixed[...] = jnp.concatenate(folded, axis=0)
        share = [mixed[pl.ds(head, group, stride=head_count), :] for head in range(head_count)]
        share = jnp.concatenate(share, axis=1).astype(jnp.bfloat16)
        to_c, to_y = at // 2, at % 2
        for zx in range(8):
            out_ref[to_y * 16 + zx * 2 + to_c] = share
        if at + 1 < len(groups):
            weighed = following


def attend_shares(queries, key_cache, value_cache, new_key, new_value, lengths):
    rows, width = queries.shape
    smem, hbm = pl.BlockSpec(memory_space=pltpu.SMEM), pl.BlockSpec(memory_space=pltpu.HBM)
    return pl.pallas_call(
        attend_kernel,
        out_shape=jax.ShapeDtypeStruct((32, 4, width), jnp.bfloat16),
        in_specs=[smem, *vmem(3), hbm, hbm],
        out_specs=pl.BlockSpec(memory_space=pltpu.VMEM),
        scratch_shapes=[
            pltpu.VMEM(key_cache.shape, key_cache.dtype),
            pltpu.VMEM(value_cache.shape, value_cache.dtype),
            pltpu.VMEM((rows * width // HEAD, HEAD), jnp.float32),
            pltpu.VMEM((4 * width // HEAD, HEAD), jnp.float32),
            pltpu.SemaphoreType.DMA((2, rows // 4)),
        ],
        compiler_params=pltpu.CompilerParams(vmem_limit_bytes=56 * 1024 * 1024),
        cost_estimate=cost(12e-6),
        name="attend",
    )(lengths, queries, new_key, new_value, key_cache, value_cache)


def keep_kernel(kept_own, kept_other, *rest):
    out_ref, _, turned = rest[-3:]
    y, c = lax.axis_index("y"), lax.axis_index("c")
    for at, kept in enumerate((kept_own, kept_other)):
        turned[...] = kept[...].astype(jnp.float32).T
        for b in range(turned.shape[0] // 16):
            both = turned[pl.ds(pl.multiple_of(b * 16 + 8 * c, 8), 8), :]
            out_ref[at, 4 * b : 4 * b + 4, :] = jnp.where(y == 0, both[:4], both[4:])


def keep(kept_own, kept_other, ready):
    features, rows = kept_own.shape
    return pl.pallas_call(
        keep_kernel,
        out_shape=(
            jax.ShapeDtypeStruct((2, rows // 4, features), jnp.float32),
            jax.ShapeDtypeStruct((8, 128), jnp.float32),
        ),
        in_specs=vmem(2) + [pl.BlockSpec(memory_space=pl.ANY)] * len(ready),
        out_specs=(*vmem(1), pl.BlockSpec(memory_space=pl.ANY)),
        scratch_shapes=[pltpu.VMEM((rows, features), jnp.float32)],
        compiler_params=pltpu.CompilerParams(vmem_limit_bytes=4 * 1024 * 1024),
        cost_estimate=cost(1e-6),
        name="keep",
    )(kept_own, kept_other, *ready)


def after(value, *others):
    def kernel(*refs):
        pass

    anywhere = pl.BlockSpec(memory_space=pl.ANY)
    return pl.pallas_call(
        kernel,
        out_shape=jax.ShapeDtypeStruct(value.shape, value.dtype),
        in_specs=[anywhere] * (1 + len(others)),
        out_specs=anywhere,
        input_output_aliases={0: 0},
        compiler_params=pltpu.CompilerParams(vmem_limit_bytes=1024 * 1024),
        name="after",
    )(value, *others)


def project_near_kernel(taken, weight_own, weight_other, kept, out_ref, far_ref, rows):
    y = lax.axis_index("y")
    blocks, share = taken.shape[0] // 2, taken.shape[1]
    for b in range(blocks):
        rows[0, b * share : (b + 1) * share, :] = taken[y * blocks + b].astype(jnp.float32)
        rows[1, b * share : (b + 1) * share, :] = taken[(1 - y) * blocks + b].astype(jnp.float32)
    far_ref[...] = rows[1].astype(jnp.bfloat16)
    near = rows[0].astype(jnp.bfloat16)
    for at, weight in enumerate((weight_own, weight_other)):
        out_ref[at] = kept[at] + lax.dot_general(near, weight[...], ACROSS, preferred_element_type=jnp.float32)


def project_far_kernel(far, weight_own, weight_other, near, out_ref):
    rows = far[...]
    own = near[0] + lax.dot_general(rows, weight_own[...], ACROSS, preferred_element_type=jnp.float32)
    other = near[1] + lax.dot_general(rows, weight_other[...], ACROSS, preferred_element_type=jnp.float32)
    core = lax.axis_index("c")
    first, second = jnp.where(core == 0, own, other), jnp.where(core == 0, other, own)
    stream = jnp.concatenate([first, second], axis=1).astype(jnp.bfloat16)
    half = stream.shape[0] // 2
    out_ref[0] = stream[:half]
    out_ref[1] = stream[half:]


def project_near(taken, weight_own, weight_other, kept):
    depth = taken.shape[2]
    rows = kept.shape[1]
    return pl.pallas_call(
        project_near_kernel,
        out_shape=(
            jax.ShapeDtypeStruct(kept.shape, jnp.float32),
            jax.ShapeDtypeStruct((rows, depth), taken.dtype),
        ),
        in_specs=vmem(4),
        out_specs=tuple(vmem(2)),
        scratch_shapes=[pltpu.VMEM((2, rows, depth), jnp.float32)],
        compiler_params=pltpu.CompilerParams(vmem_limit_bytes=16 * 1024 * 1024),
        cost_estimate=cost(2e-6),
        name="project_near",
    )(taken, weight_own, weight_other, kept)


def project_far(far, weight_own, weight_other, near):
    rows, width = near.shape[1:]
    return pl.pallas_call(
        project_far_kernel,
        out_shape=jax.ShapeDtypeStruct((2, rows // 2, 2 * width), jnp.bfloat16),
        in_specs=vmem(4),
        out_specs=pl.BlockSpec(memory_space=pltpu.VMEM),
        compiler_params=pltpu.CompilerParams(vmem_limit_bytes=16 * 1024 * 1024),
        cost_estimate=cost(2e-6),
        name="project_far",
    )(far, weight_own, weight_other, near)


def pre_activations(rows, weights):
    block = rows[0].shape[1]
    main = block // 256 * 256
    rest = jnp.concatenate([row[:, main:] for row in rows], axis=1)
    sums = []
    for half in range(2):
        total = None
        for dz, row in enumerate(rows):
            part = jnp.dot(row[:, :main], weights[half, dz, :main, :], preferred_element_type=jnp.float32)
            total = part if total is None else total + part
        ends = jnp.concatenate([weights[half, dz, main:, :] for dz in range(4)], axis=0)
        sums.append(total + jnp.dot(rest, ends, preferred_element_type=jnp.float32))
    return sums


def encode_first_kernel(own, other, own_far, other_far, enc_own, enc_other, out_ref, later_ref, weights, arrived):
    z, x = lax.axis_index("z"), lax.axis_index("x")
    block = own.shape[3]
    pairs = ((own, other), (own_far, other_far))
    now, later = [], []
    for half, enc in enumerate((enc_own, enc_other)):
        for dz in range(4):
            for dx, to, copies in ((0, weights, now), (1, later_ref, later)):
                start = pl.multiple_of(((z ^ dz) * 2 + (x ^ dx)) * block, 64)
                sem = arrived.at[dx, half * 4 + dz]
                copies.append(pltpu.make_async_copy(enc.at[pl.ds(start, block)], to.at[half, dz], sem))
    for copy in now + later:
        copy.start()
    for copy in now:
        copy.wait()
    rows = [
        jnp.concatenate([piece[half, dz] for piece in pair for half in range(2)], axis=0)
        for pair in pairs
        for dz in range(2)
    ]
    sums = pre_activations(rows, weights)
    out_ref[0] = sums[0]
    out_ref[1] = sums[1]
    for copy in later:
        copy.wait()


def encode_second_kernel(
    own,
    upper,
    lower,
    own_far,
    upper_far,
    lower_far,
    first,
    weights,
    bias_own,
    code_own,
    probe_own,
    bias_other,
    code_other,
    probe_other,
    out_ref,
    ordered,
):
    rows = [
        jnp.concatenate([piece[0, dz], piece[1, dz], up[dz], low[dz]], axis=0)
        for piece, up, low in ((own, upper, lower), (own_far, upper_far, lower_far))
        for dz in range(2)
    ]
    sums = pre_activations(rows, weights)
    partial = None
    halves = ((bias_own, code_own, probe_own), (bias_other, code_other, probe_other))
    for at, (bias, code, probe) in enumerate(halves):
        pre = sums[at] + first[at] + bias[...]
        threshold = code[...].astype(jnp.float32) / 16.0
        ramped = jnp.clip((pre - threshold) / RAMP_WIDTH, 0.0, 1.0)
        active = (pre * ramped).astype(jnp.bfloat16)
        probed = jnp.dot(active, probe[...], preferred_element_type=jnp.float32)
        partial = probed if partial is None else partial + probed
    for half in range(2):
        for b in range(16):
            at = half * 64 + b * 4
            ordered[b, 4 * half : 4 * half + 4, :] = partial[at : at + 4, :]
    out_ref[...] = ordered[...].astype(jnp.bfloat16)


def encode_first(near, far, enc):
    own = near[0]
    rows, block, latents = 4 * own.shape[2], own.shape[3], enc[0].shape[1]
    weights = (2, 4, block, latents)
    hbm = pl.BlockSpec(memory_space=pltpu.HBM)
    return pl.pallas_call(
        encode_first_kernel,
        out_shape=(
            jax.ShapeDtypeStruct((2, rows, latents), jnp.float32),
            jax.ShapeDtypeStruct(weights, enc[0].dtype),
        ),
        in_specs=[*vmem(4), hbm, hbm],
        out_specs=tuple(vmem(2)),
        scratch_shapes=[pltpu.VMEM(weights, enc[0].dtype), pltpu.SemaphoreType.DMA((2, 8))],
        compiler_params=pltpu.CompilerParams(vmem_limit_bytes=50 * 1024 * 1024),
        cost_estimate=cost(2e-6),
        name="encode_first",
    )(*near, *far, *enc)


def encode_second(near, far, first, weights, own, other):
    columns = own[2].shape[1]
    return pl.pallas_call(
        encode_second_kernel,
        out_shape=jax.ShapeDtypeStruct((16, 8, columns), jnp.bfloat16),
        in_specs=vmem(14),
        out_specs=pl.BlockSpec(memory_space=pltpu.VMEM),
        scratch_shapes=[pltpu.VMEM((16, 8, columns), jnp.float32)],
        compiler_params=pltpu.CompilerParams(vmem_limit_bytes=24 * 1024 * 1024),
        cost_estimate=cost(2e-6),
        name="encode_second",
    )(*near, *far, first, weights, *own, *other)


def finish_kernel(parts, probe_bias, head_weight, head_bias, scores_ref, logits_ref):
    sums = parts[...].astype(jnp.float32)
    first = jnp.sum(sums[:8], axis=0)
    second = jnp.sum(sums[8:], axis=0)
    scores = first + jnp.concatenate([second[4:], second[:4]], axis=0) + probe_bias[...]
    scores_ref[...] = scores
    gated = scores / (1.0 + jnp.exp(-scores))
    logits_ref[...] = (
        lax.dot_general(
            gated,
            head_weight[...],
            (((1,), (1,)), ((), ())),
            precision=lax.Precision.HIGHEST,
            preferred_element_type=jnp.float32,
        )
        + head_bias[...]
    )


def finish(parts, probe_bias, head_weight, head_bias):
    rows, columns = parts.shape[1:]
    return pl.pallas_call(
        finish_kernel,
        out_shape=(
            jax.ShapeDtypeStruct((rows, columns), jnp.float32),
            jax.ShapeDtypeStruct((rows, head_weight.shape[1]), jnp.float32),
        ),
        in_specs=vmem(4),
        out_specs=tuple(vmem(2)),
        compiler_params=pltpu.CompilerParams(vmem_limit_bytes=8 * 1024 * 1024),
        name="finish",
    )(parts, probe_bias.reshape(1, -1), head_weight.T, head_bias.reshape(1, -1))


def chip_body(
    queries,
    key_cache,
    value_cache,
    new_key,
    new_value,
    lengths,
    out_proj,
    residual,
    enc_weight,
    enc_bias,
    threshold_code,
    probe_weight,
    probe_bias,
    head_weight,
    head_bias,
):
    proj = out_proj.T
    proj_y = xor(proj, 16)
    enc_other = xor(enc_weight, 1)
    proj_c = xor(proj, 1)
    probe_other = xor(probe_weight, 1)
    bias_other, code_other = xor(enc_bias, 1), xor(threshold_code, 1)
    kept = residual.T
    kept_other = xor(kept, 1)

    sent = attend_shares(queries, key_cache, value_cache, new_key, new_value, lengths)
    kept_rows, token = keep(kept, kept_other, (probe_other, bias_other, code_other))
    taken = lax.all_to_all(sent, ALL, 0, 0, tiled=True)
    proj_y = after(proj_y, taken, token)
    proj_yc = xor(proj_y, 1)
    near, far = project_near(taken, proj, proj_c, kept_rows)
    stream = project_far(far, proj_y, proj_yc, near)
    along_z = [stream, xor(stream, 4), xor(stream, 8), xor(stream, 12)]

    def spread(mine):
        over_y, over_x = xor(mine, 16), xor(mine, 2)
        return (mine, over_y), (over_x, xor(over_x[0], 16), xor(over_y[1], 2))

    first_near, second_near = spread(jnp.stack(along_z[:2], axis=1))
    first_far, second_far = spread(after(jnp.stack(along_z[2:], axis=1), second_near[0]))
    first, weights = encode_first(first_near, first_far, (enc_weight, enc_other))
    partial = encode_second(
        second_near,
        second_far,
        first,
        weights,
        (enc_bias[None], threshold_code[None], probe_weight),
        (bias_other[None], code_other[None], probe_other),
    )
    parts = lax.all_to_all(partial, PLANE, 0, 0, tiled=True)
    return finish(parts, probe_bias, head_weight, head_bias)


def body(
    queries,
    key_cache,
    value_cache,
    new_key,
    new_value,
    lengths,
    out_proj,
    residual,
    enc_weight,
    enc_bias,
    threshold_code,
    probe_weight,
    probe_bias,
    head_weight,
    head_bias,
):
    attended = attend(queries, key_cache, value_cache, new_key, new_value, lengths)
    partial_heads = jnp.dot(
        lax.all_gather(attended, "lat", axis=0, tiled=True),
        out_proj,
        preferred_element_type=jnp.float32,
    )
    projected = lax.psum(partial_heads, "tp")
    stream = (residual.astype(jnp.float32) + projected).astype(jnp.bfloat16)
    pre_act = jnp.dot(
        lax.all_gather(stream, "lat", axis=1, tiled=True),
        enc_weight,
        preferred_element_type=jnp.float32,
    )
    pre_act = pre_act + enc_bias
    threshold = threshold_code.astype(jnp.float32) / 16.0
    ramped = jnp.clip((pre_act - threshold) / RAMP_WIDTH, 0.0, 1.0)
    activations = (pre_act * ramped).astype(jnp.bfloat16)
    halfway = lax.psum_scatter(
        jnp.dot(activations, probe_weight, preferred_element_type=jnp.float32),
        "tp",
        scatter_dimension=0,
        tiled=True,
    )
    summed = lax.psum_scatter(halfway, "lat", scatter_dimension=0, tiled=True)
    probe_scores = summed + probe_bias
    harm_logits = (
        jnp.dot(
            jax.nn.silu(probe_scores),
            head_weight,
            precision=lax.Precision.HIGHEST,
            preferred_element_type=jnp.float32,
        )
        + head_bias
    )
    return (probe_scores, harm_logits)


def solution(mesh):
    chips = mesh.shape["tp"] == 2 and mesh.shape["lat"] == 16
    tp, lat = "tp", "lat"
    if chips:
        mesh = Mesh(mesh.devices.reshape(2, 4, 2, 2), ALL)
        tp, lat = ("y",), ("z", "x", "c")
    both = ALL if chips else ("tp", "lat")
    in_specs = (
        P(lat, tp),
        P(lat, None, tp),
        P(lat, None, tp),
        P(lat, tp),
        P(lat, tp),
        P(lat),
        P(tp, lat),
        P(None, lat),
        P(None, both),
        P(both),
        P(both),
        P(both, None),
        P(),
        P(),
        P(),
    )
    out_specs = (P(both, None), P(both, None))
    return jax.shard_map(
        chip_body if chips else body, mesh=mesh, in_specs=in_specs, out_specs=out_specs, check_vma=False
    )
```

```python
import jax
import jax.numpy as jnp
from jax import lax
from jax.experimental import pallas as pl
from jax.experimental.pallas import tpu as pltpu
from jax.sharding import Mesh, PartitionSpec as P

HEAD = 128


SOFT_CAP = 50.0
QUERY_SCALE = 1.0 / 12.0
RAMP_WIDTH = 0.25
ACROSS = (((1,), (1,)), ((), ()))

ALL = ("y", "z", "x", "c")
ODD_FIRST = [*range(1, 32, 2), *range(0, 32, 2)]
PLANES = [list(range(30 + core, -1, -2)) for core in range(2)]


def attend(queries, key_cache, value_cache, new_key, new_value, lengths):
    row_count, positions, kv_width = key_cache.shape
    kv_heads = kv_width // HEAD
    group_size = queries.shape[1] // kv_width
    grouped = queries.reshape(row_count, kv_heads, group_size, HEAD)
    key_rows = key_cache.reshape(row_count, positions, kv_heads, HEAD)
    values = value_cache.reshape(row_count, positions, kv_heads, HEAD)
    fresh_key = new_key.reshape(row_count, kv_heads, HEAD)
    fresh_value = new_value.reshape(row_count, kv_heads, 1, HEAD).astype(jnp.float32)
    cached = jnp.einsum("rkgd,rlkd->rkgl", grouped, key_rows, preferred_element_type=jnp.float32)
    own_score = jnp.einsum("rkgd,rkd->rkg", grouped, fresh_key, preferred_element_type=jnp.float32)
    cached = SOFT_CAP * jnp.tanh(cached * (QUERY_SCALE / SOFT_CAP))
    own_score = SOFT_CAP * jnp.tanh(own_score * (QUERY_SCALE / SOFT_CAP))
    live_mask = jnp.arange(positions, dtype=jnp.int32)[None, :] < lengths[:, None]
    cached_exp = jnp.where(live_mask[:, None, None, :], jnp.exp(cached), 0.0)
    own_exp = jnp.exp(own_score)
    denominator = jnp.sum(cached_exp, axis=-1) + own_exp
    cached_weight = (cached_exp / denominator[..., None]).astype(jnp.bfloat16)
    own_weight = (own_exp / denominator).astype(jnp.bfloat16)
    mixture = jnp.einsum(
        "rkgl,rlkd->rkgd", cached_weight, values, preferred_element_type=jnp.float32
    )
    mixture = mixture + own_weight.astype(jnp.float32)[..., None] * fresh_value
    return mixture.reshape(row_count, kv_heads * group_size * HEAD).astype(jnp.bfloat16)


def xor(value, bits):
    return lax.ppermute(value, ALL, [(i, i ^ bits) for i in range(32)])


def cost(seconds):
    return pl.CostEstimate(flops=0, bytes_accessed=int(seconds * 3.69e12), transcendentals=0)


def vmem(count):
    return [pl.BlockSpec(memory_space=pltpu.VMEM)] * count


def attend_kernel(
    lengths,
    queries,
    new_key,
    new_value,
    keys_at,
    values_at,
    out_ref,
    keys,
    values,
    heads,
    mixed,
    arrived,
):
    row_count, positions, kv_width = keys.shape
    head_count = queries.shape[1] // HEAD
    kv_heads = kv_width // HEAD
    group = 4
    groups = [range(at, at + group) for at in range(0, row_count, group)]
    copies = []
    for at in range(len(groups)):
        rows = pl.ds(at * group, group)
        copies.append(
            (
                pltpu.make_async_copy(keys_at.at[rows], keys.at[rows], arrived.at[0, at]),
                pltpu.make_async_copy(values_at.at[rows], values.at[rows], arrived.at[1, at]),
            )
        )
    copies[0][0].start()
    for at in range(len(groups)):
        if at + 1 < len(groups):
            copies[at + 1][0].start()
        copies[at][1].start()
    for head in range(head_count):
        heads[pl.ds(head, row_count, stride=head_count), :] = queries[:, head * HEAD : (head + 1) * HEAD].astype(
            jnp.float32
        )
    shape = (head_count, kv_width)
    of_head = lax.broadcasted_iota(jnp.int32, shape, 0) // (head_count // kv_heads)
    in_block = of_head == lax.broadcasted_iota(jnp.int32, shape, 1) // HEAD
    place = lax.broadcasted_iota(jnp.int32, (head_count, positions), 1)
    fresh_key = new_key[...].astype(jnp.float32)
    fresh_value = new_value[...].astype(jnp.float32)

    def cap(score):
        return jnp.exp(SOFT_CAP * jnp.tanh(score * (QUERY_SCALE / SOFT_CAP)))

    def weigh(row):
        query = heads[row * head_count : (row + 1) * head_count, :]
        spread = jnp.where(in_block, jnp.concatenate([query] * kv_heads, axis=1), 0.0)
        scores = lax.dot_general(
            spread.astype(jnp.bfloat16), keys[row], ACROSS, preferred_element_type=jnp.float32
        )
        own = cap(jnp.sum(spread * fresh_key[row : row + 1, :], axis=1, keepdims=True))
        exps = jnp.where(place < lengths[row], cap(scores), 0.0)
        scale = 1.0 / (jnp.sum(exps, axis=1, keepdims=True) + own)
        return (exps * scale).astype(jnp.bfloat16), (own * scale).astype(jnp.bfloat16).astype(jnp.float32)

    def mix(row, weights, own_weight):
        mixture = jnp.dot(weights, values[row], preferred_element_type=jnp.float32)
        mixture = jnp.where(in_block, mixture + own_weight * fresh_value[row : row + 1, :], 0.0)
        folded = mixture[:, :HEAD]
        for kv_head in range(1, kv_heads):
            folded = folded + mixture[:, kv_head * HEAD : (kv_head + 1) * HEAD]
        return folded

    copies[0][0].wait()
    weighed = [weigh(row) for row in groups[0]]
    for at in range(len(groups)):
        copies[at][1].wait()
        if at + 1 < len(groups):
            copies[at + 1][0].wait()
            following = [weigh(row) for row in groups[at + 1]]
        folded = [mix(row, *weighed[nth]) for nth, row in enumerate(groups[at])]
        mixed[...] = jnp.concatenate(folded, axis=0)
        share = [mixed[pl.ds(head, group, stride=head_count), :] for head in range(head_count)]
        share = jnp.concatenate(share, axis=1).astype(jnp.bfloat16)
        to_c, to_y = at // 2, at % 2
        for zx in range(8):
            out_ref[(1 - to_c) * 16 + to_y * 8 + zx] = share
        if at + 1 < len(groups):
            weighed = following


def attend_shares(queries, key_cache, value_cache, new_key, new_value, lengths):
    rows, width = queries.shape
    smem, hbm = pl.BlockSpec(memory_space=pltpu.SMEM), pl.BlockSpec(memory_space=pltpu.HBM)
    return pl.pallas_call(
        attend_kernel,
        out_shape=jax.ShapeDtypeStruct((32, 4, width), jnp.bfloat16),
        in_specs=[smem, *vmem(3), hbm, hbm],
        out_specs=pl.BlockSpec(memory_space=pltpu.VMEM),
        scratch_shapes=[
            pltpu.VMEM(key_cache.shape, key_cache.dtype),
            pltpu.VMEM(value_cache.shape, value_cache.dtype),
            pltpu.VMEM((rows * width // HEAD, HEAD), jnp.float32),
            pltpu.VMEM((4 * width // HEAD, HEAD), jnp.float32),
            pltpu.SemaphoreType.DMA((2, rows // 4)),
        ],
        compiler_params=pltpu.CompilerParams(vmem_limit_bytes=56 * 1024 * 1024),
        cost_estimate=cost(12e-6),
        name="attend",
    )(lengths, queries, new_key, new_value, key_cache, value_cache)


def keep_kernel(kept_own, kept_other, *rest):
    out_ref, _, turned = rest[-3:]
    y, c = lax.axis_index("y"), lax.axis_index("c")
    for at, kept in enumerate((kept_own, kept_other)):
        turned[...] = kept[...].astype(jnp.float32).T
        for b in range(turned.shape[0] // 16):
            both = turned[pl.ds(pl.multiple_of(b * 16 + 8 * c, 8), 8), :]
            out_ref[at, 4 * b : 4 * b + 4, :] = jnp.where(y == 0, both[:4], both[4:])


def keep(kept_own, kept_other, ready):
    features, rows = kept_own.shape
    return pl.pallas_call(
        keep_kernel,
        out_shape=(
            jax.ShapeDtypeStruct((2, rows // 4, features), jnp.float32),
            jax.ShapeDtypeStruct((8, 128), jnp.float32),
        ),
        in_specs=vmem(2) + [pl.BlockSpec(memory_space=pl.ANY)] * len(ready),
        out_specs=(*vmem(1), pl.BlockSpec(memory_space=pl.ANY)),
        scratch_shapes=[pltpu.VMEM((rows, features), jnp.float32)],
        compiler_params=pltpu.CompilerParams(vmem_limit_bytes=4 * 1024 * 1024),
        cost_estimate=cost(1e-6),
        name="keep",
    )(kept_own, kept_other, *ready)


def after(value, *others):
    def kernel(*refs):
        pass

    anywhere = pl.BlockSpec(memory_space=pl.ANY)
    return pl.pallas_call(
        kernel,
        out_shape=jax.ShapeDtypeStruct(value.shape, value.dtype),
        in_specs=[anywhere] * (1 + len(others)),
        out_specs=anywhere,
        input_output_aliases={0: 0},
        compiler_params=pltpu.CompilerParams(vmem_limit_bytes=1024 * 1024),
        name="after",
    )(value, *others)


def project_kernel(taken, near_own, near_other, far_own, kept, *rest):
    far_other, (out_ref, rows) = rest[:-2], rest[-2:]
    y, core = lax.axis_index("y"), lax.axis_index("c")
    blocks, share = taken.shape[0] // 2, taken.shape[1]
    for b in range(blocks):
        at = (1 - b % 2) * blocks + b // 2
        rows[0, b * share : (b + 1) * share, :] = taken[at + y * 8].astype(jnp.float32)
        rows[1, b * share : (b + 1) * share, :] = taken[at + (1 - y) * 8].astype(jnp.float32)
    near, far = rows[0].astype(jnp.bfloat16), rows[1].astype(jnp.bfloat16)

    def across(left, right):
        return lax.dot_general(left, right, ACROSS, preferred_element_type=jnp.float32)

    own = kept[0] + across(near, near_own[...]) + across(far, far_own[...])
    other = kept[1] + across(near, near_other[...])
    depth = far_other[0].shape[1]
    for at, piece in enumerate(far_other):
        other += across(far[:, at * depth : (at + 1) * depth], piece[...])
    first, second = jnp.where(core == 0, own, other), jnp.where(core == 0, other, own)
    stream = jnp.concatenate([first, second], axis=1).astype(jnp.bfloat16)
    half = stream.shape[0] // 2
    out_ref[0] = stream[:half]
    out_ref[1] = stream[half:]


def project(taken, near_own, near_other, far_own, far_other, kept):
    depth = taken.shape[2]
    rows, width = kept.shape[1:]
    return pl.pallas_call(
        project_kernel,
        out_shape=jax.ShapeDtypeStruct((2, rows // 2, 2 * width), jnp.bfloat16),
        in_specs=vmem(5 + len(far_other)),
        out_specs=pl.BlockSpec(memory_space=pltpu.VMEM),
        scratch_shapes=[pltpu.VMEM((2, rows, depth), jnp.float32)],
        compiler_params=pltpu.CompilerParams(vmem_limit_bytes=16 * 1024 * 1024),
        cost_estimate=cost(2e-6),
        name="project",
    )(taken, near_own, near_other, far_own, kept, *far_other)


def pre_activations(rows, weights):
    block = rows[0].shape[1]
    main = block // 256 * 256
    rest = jnp.concatenate([row[:, main:] for row in rows], axis=1)
    sums = []
    for half in range(2):
        total = None
        for dz, row in enumerate(rows):
            part = jnp.dot(row[:, :main], weights[half, dz, :main, :], preferred_element_type=jnp.float32)
            total = part if total is None else total + part
        ends = jnp.concatenate([weights[half, dz, main:, :] for dz in range(4)], axis=0)
        sums.append(total + jnp.dot(rest, ends, preferred_element_type=jnp.float32))
    return sums


def encode_first_kernel(own, other, own_far, other_far, enc_own, enc_other, out_ref, later_ref, weights, arrived):
    z, x = lax.axis_index("z"), lax.axis_index("x")
    block = own.shape[3]
    pairs = ((own, other), (own_far, other_far))
    now, later = [], []
    for half, enc in enumerate((enc_own, enc_other)):
        for dz in range(4):
            for dx, to, copies in ((0, weights, now), (1, later_ref, later)):
                start = pl.multiple_of(((z ^ dz) * 2 + (x ^ dx)) * block, 64)
                sem = arrived.at[dx, half * 4 + dz]
                copies.append(pltpu.make_async_copy(enc.at[pl.ds(start, block)], to.at[half, dz], sem))
    for copy in now + later:
        copy.start()
    for copy in now:
        copy.wait()
    rows = [
        jnp.concatenate([piece[half, dz] for piece in pair for half in range(2)], axis=0)
        for pair in pairs
        for dz in range(2)
    ]
    sums = pre_activations(rows, weights)
    out_ref[0] = sums[0]
    out_ref[1] = sums[1]
    for copy in later:
        copy.wait()


def encode_second_kernel(
    own,
    upper,
    lower,
    own_far,
    upper_far,
    lower_far,
    first,
    weights,
    bias_own,
    code_own,
    probe_own,
    bias_other,
    code_other,
    probe_other,
    out_ref,
    ordered,
):
    rows = [
        jnp.concatenate([piece[0, dz], piece[1, dz], up[dz], low[dz]], axis=0)
        for piece, up, low in ((own, upper, lower), (own_far, upper_far, lower_far))
        for dz in range(2)
    ]
    sums = pre_activations(rows, weights)
    partial = None
    halves = ((bias_own, code_own, probe_own), (bias_other, code_other, probe_other))
    for at, (bias, code, probe) in enumerate(halves):
        pre = sums[at] + first[at] + bias[...]
        threshold = code[...].astype(jnp.float32) / 16.0
        ramped = jnp.clip((pre - threshold) / RAMP_WIDTH, 0.0, 1.0)
        active = (pre * ramped).astype(jnp.bfloat16)
        probed = jnp.dot(active, probe[...], preferred_element_type=jnp.float32)
        partial = probed if partial is None else partial + probed
    for half in range(2):
        for b in range(16):
            at = half * 64 + b * 4
            ordered[15 - b, 4 * half : 4 * half + 4, :] = partial[at : at + 4, :]
    out_ref[...] = ordered[...].astype(jnp.bfloat16)


def encode_first(near, far, enc):
    own = near[0]
    rows, block, latents = 4 * own.shape[2], own.shape[3], enc[0].shape[1]
    weights = (2, 4, block, latents)
    hbm = pl.BlockSpec(memory_space=pltpu.HBM)
    return pl.pallas_call(
        encode_first_kernel,
        out_shape=(
            jax.ShapeDtypeStruct((2, rows, latents), jnp.float32),
            jax.ShapeDtypeStruct(weights, enc[0].dtype),
        ),
        in_specs=[*vmem(4), hbm, hbm],
        out_specs=tuple(vmem(2)),
        scratch_shapes=[pltpu.VMEM(weights, enc[0].dtype), pltpu.SemaphoreType.DMA((2, 8))],
        compiler_params=pltpu.CompilerParams(vmem_limit_bytes=50 * 1024 * 1024),
        cost_estimate=cost(2e-6),
        name="encode_first",
    )(*near, *far, *enc)


def encode_second(near, far, first, weights, own, other):
    columns = own[2].shape[1]
    return pl.pallas_call(
        encode_second_kernel,
        out_shape=jax.ShapeDtypeStruct((16, 8, columns), jnp.bfloat16),
        in_specs=vmem(14),
        out_specs=pl.BlockSpec(memory_space=pltpu.VMEM),
        scratch_shapes=[pltpu.VMEM((16, 8, columns), jnp.float32)],
        compiler_params=pltpu.CompilerParams(vmem_limit_bytes=24 * 1024 * 1024),
        cost_estimate=cost(2e-6),
        name="encode_second",
    )(*near, *far, first, weights, *own, *other)


def finish_kernel(parts, probe_bias, head_weight, head_bias, scores_ref, logits_ref):
    sums = parts[...].astype(jnp.float32)
    first = jnp.sum(sums[8:], axis=0)
    second = jnp.sum(sums[:8], axis=0)
    scores = first + jnp.concatenate([second[4:], second[:4]], axis=0) + probe_bias[...]
    scores_ref[...] = scores
    gated = scores / (1.0 + jnp.exp(-scores))
    logits_ref[...] = (
        lax.dot_general(
            gated,
            head_weight[...],
            (((1,), (1,)), ((), ())),
            precision=lax.Precision.HIGHEST,
            preferred_element_type=jnp.float32,
        )
        + head_bias[...]
    )


def finish(parts, probe_bias, head_weight, head_bias):
    rows, columns = parts.shape[1:]
    return pl.pallas_call(
        finish_kernel,
        out_shape=(
            jax.ShapeDtypeStruct((rows, columns), jnp.float32),
            jax.ShapeDtypeStruct((rows, head_weight.shape[1]), jnp.float32),
        ),
        in_specs=vmem(4),
        out_specs=tuple(vmem(2)),
        compiler_params=pltpu.CompilerParams(vmem_limit_bytes=8 * 1024 * 1024),
        name="finish",
    )(parts, probe_bias.reshape(1, -1), head_weight.T, head_bias.reshape(1, -1))


def chip_body(
    queries,
    key_cache,
    value_cache,
    new_key,
    new_value,
    lengths,
    out_proj,
    residual,
    enc_weight,
    enc_bias,
    threshold_code,
    probe_weight,
    probe_bias,
    head_weight,
    head_bias,
):
    proj = out_proj.T
    proj_y = xor(proj, 16)
    enc_other = xor(enc_weight, 1)
    proj_c = xor(proj, 1)
    probe_other = xor(probe_weight, 1)
    bias_other, code_other = xor(enc_bias, 1), xor(threshold_code, 1)
    kept = residual.T
    kept_other = xor(kept, 1)

    sent = attend_shares(queries, key_cache, value_cache, new_key, new_value, lengths)
    kept_rows, token = keep(kept, kept_other, ())
    taken = lax.all_to_all(sent, ALL, 0, 0, tiled=True, axis_index_groups=[ODD_FIRST])
    proj_y = after(proj_y, token)
    depth = proj_y.shape[1] // 4
    proj_yc = [xor(proj_y[:, at : at + depth], 1) for at in range(0, proj_y.shape[1], depth)]
    taken = after(taken, *proj_yc, probe_other, bias_other, code_other)
    stream = project(taken, proj, proj_c, proj_y, proj_yc, kept_rows)
    along_z = [stream, xor(stream, 4), xor(stream, 8), xor(stream, 12)]

    def spread(mine):
        over_y, over_x = xor(mine, 16), xor(mine, 2)
        return (mine, over_y), (over_x, xor(over_x[0], 16), xor(over_y[1], 2))

    first_near, second_near = spread(jnp.stack(along_z[:2], axis=1))
    first_far, second_far = spread(after(jnp.stack(along_z[2:], axis=1), second_near[0]))
    first, weights = encode_first(first_near, first_far, (enc_weight, enc_other))
    partial = encode_second(
        second_near,
        second_far,
        first,
        weights,
        (enc_bias[None], threshold_code[None], probe_weight),
        (bias_other[None], code_other[None], probe_other),
    )
    parts = lax.all_to_all(partial, ALL, 0, 0, tiled=True, axis_index_groups=PLANES)
    return finish(parts, probe_bias, head_weight, head_bias)


def body(
    queries,
    key_cache,
    value_cache,
    new_key,
    new_value,
    lengths,
    out_proj,
    residual,
    enc_weight,
    enc_bias,
    threshold_code,
    probe_weight,
    probe_bias,
    head_weight,
    head_bias,
):
    attended = attend(queries, key_cache, value_cache, new_key, new_value, lengths)
    partial_heads = jnp.dot(
        lax.all_gather(attended, "lat", axis=0, tiled=True),
        out_proj,
        preferred_element_type=jnp.float32,
    )
    projected = lax.psum(partial_heads, "tp")
    stream = (residual.astype(jnp.float32) + projected).astype(jnp.bfloat16)
    pre_act = jnp.dot(
        lax.all_gather(stream, "lat", axis=1, tiled=True),
        enc_weight,
        preferred_element_type=jnp.float32,
    )
    pre_act = pre_act + enc_bias
    threshold = threshold_code.astype(jnp.float32) / 16.0
    ramped = jnp.clip((pre_act - threshold) / RAMP_WIDTH, 0.0, 1.0)
    activations = (pre_act * ramped).astype(jnp.bfloat16)
    halfway = lax.psum_scatter(
        jnp.dot(activations, probe_weight, preferred_element_type=jnp.float32),
        "tp",
        scatter_dimension=0,
        tiled=True,
    )
    summed = lax.psum_scatter(halfway, "lat", scatter_dimension=0, tiled=True)
    probe_scores = summed + probe_bias
    harm_logits = (
        jnp.dot(
            jax.nn.silu(probe_scores),
            head_weight,
            precision=lax.Precision.HIGHEST,
            preferred_element_type=jnp.float32,
        )
        + head_bias
    )
    return (probe_scores, harm_logits)


def solution(mesh):
    chips = mesh.shape["tp"] == 2 and mesh.shape["lat"] == 16
    tp, lat = "tp", "lat"
    if chips:
        mesh = Mesh(mesh.devices.reshape(2, 4, 2, 2), ALL)
        tp, lat = ("y",), ("z", "x", "c")
    both = ALL if chips else ("tp", "lat")
    in_specs = (
        P(lat, tp),
        P(lat, None, tp),
        P(lat, None, tp),
        P(lat, tp),
        P(lat, tp),
        P(lat),
        P(tp, lat),
        P(None, lat),
        P(None, both),
        P(both),
        P(both),
        P(both, None),
        P(),
        P(),
        P(),
    )
    out_specs = (P(both, None), P(both, None))
    return jax.shard_map(
        chip_body if chips else body, mesh=mesh, in_specs=in_specs, out_specs=out_specs, check_vma=False
    )
```

```python
import jax
import jax.numpy as jnp
from jax import lax
from jax.experimental import pallas as pl
from jax.experimental.pallas import tpu as pltpu
from jax.sharding import Mesh, PartitionSpec as P

HEAD = 128


SOFT_CAP = 50.0
QUERY_SCALE = 1.0 / 12.0
RAMP_WIDTH = 0.25
ACROSS = (((1,), (1,)), ((), ()))

ALL = ("y", "z", "x", "c")
ORDER = [*range(1, 32, 2), *range(0, 32, 2)]
PLANES = [list(range(30 + core, -1, -2)) for core in range(2)]


def attend(queries, key_cache, value_cache, new_key, new_value, lengths):
    row_count, positions, kv_width = key_cache.shape
    kv_heads = kv_width // HEAD
    group_size = queries.shape[1] // kv_width
    grouped = queries.reshape(row_count, kv_heads, group_size, HEAD)
    key_rows = key_cache.reshape(row_count, positions, kv_heads, HEAD)
    values = value_cache.reshape(row_count, positions, kv_heads, HEAD)
    fresh_key = new_key.reshape(row_count, kv_heads, HEAD)
    fresh_value = new_value.reshape(row_count, kv_heads, 1, HEAD).astype(jnp.float32)
    cached = jnp.einsum("rkgd,rlkd->rkgl", grouped, key_rows, preferred_element_type=jnp.float32)
    own_score = jnp.einsum("rkgd,rkd->rkg", grouped, fresh_key, preferred_element_type=jnp.float32)
    cached = SOFT_CAP * jnp.tanh(cached * (QUERY_SCALE / SOFT_CAP))
    own_score = SOFT_CAP * jnp.tanh(own_score * (QUERY_SCALE / SOFT_CAP))
    live_mask = jnp.arange(positions, dtype=jnp.int32)[None, :] < lengths[:, None]
    cached_exp = jnp.where(live_mask[:, None, None, :], jnp.exp(cached), 0.0)
    own_exp = jnp.exp(own_score)
    denominator = jnp.sum(cached_exp, axis=-1) + own_exp
    cached_weight = (cached_exp / denominator[..., None]).astype(jnp.bfloat16)
    own_weight = (own_exp / denominator).astype(jnp.bfloat16)
    mixture = jnp.einsum(
        "rkgl,rlkd->rkgd", cached_weight, values, preferred_element_type=jnp.float32
    )
    mixture = mixture + own_weight.astype(jnp.float32)[..., None] * fresh_value
    return mixture.reshape(row_count, kv_heads * group_size * HEAD).astype(jnp.bfloat16)


def xor(value, bits):
    return lax.ppermute(value, ALL, [(i, i ^ bits) for i in range(32)])


def cost(seconds):
    return pl.CostEstimate(flops=0, bytes_accessed=int(seconds * 3.69e12), transcendentals=0)


def vmem(count):
    return [pl.BlockSpec(memory_space=pltpu.VMEM)] * count


def attend_kernel(
    lengths,
    queries,
    new_key,
    new_value,
    keys_at,
    values_at,
    out_ref,
    keys,
    values,
    heads,
    mixed,
    arrived,
):
    row_count, positions, kv_width = keys.shape
    head_count = queries.shape[1] // HEAD
    kv_heads = kv_width // HEAD
    group = 4
    groups = [range(at, at + group) for at in range(0, row_count, group)]
    copies = []
    for at in range(len(groups)):
        rows = pl.ds(at * group, group)
        copies.append(
            (
                pltpu.make_async_copy(keys_at.at[rows], keys.at[rows], arrived.at[0, at]),
                pltpu.make_async_copy(values_at.at[rows], values.at[rows], arrived.at[1, at]),
            )
        )
    copies[0][0].start()
    for at in range(len(groups)):
        if at + 1 < len(groups):
            copies[at + 1][0].start()
        copies[at][1].start()
    for head in range(head_count):
        heads[pl.ds(head, row_count, stride=head_count), :] = queries[:, head * HEAD : (head + 1) * HEAD].astype(
            jnp.float32
        )
    shape = (head_count, kv_width)
    of_head = lax.broadcasted_iota(jnp.int32, shape, 0) // (head_count // kv_heads)
    in_block = of_head == lax.broadcasted_iota(jnp.int32, shape, 1) // HEAD
    place = lax.broadcasted_iota(jnp.int32, (head_count, positions), 1)
    fresh_key = new_key[...].astype(jnp.float32)
    fresh_value = new_value[...].astype(jnp.float32)

    def cap(score):
        return jnp.exp(SOFT_CAP * jnp.tanh(score * (QUERY_SCALE / SOFT_CAP)))

    def weigh(row):
        query = heads[row * head_count : (row + 1) * head_count, :]
        spread = jnp.where(in_block, jnp.concatenate([query] * kv_heads, axis=1), 0.0)
        scores = lax.dot_general(
            spread.astype(jnp.bfloat16), keys[row], ACROSS, preferred_element_type=jnp.float32
        )
        own = cap(jnp.sum(spread * fresh_key[row : row + 1, :], axis=1, keepdims=True))
        exps = jnp.where(place < lengths[row], cap(scores), 0.0)
        scale = 1.0 / (jnp.sum(exps, axis=1, keepdims=True) + own)
        return (exps * scale).astype(jnp.bfloat16), (own * scale).astype(jnp.bfloat16).astype(jnp.float32)

    def mix(row, weights, own_weight):
        mixture = jnp.dot(weights, values[row], preferred_element_type=jnp.float32)
        mixture = jnp.where(in_block, mixture + own_weight * fresh_value[row : row + 1, :], 0.0)
        folded = mixture[:, :HEAD]
        for kv_head in range(1, kv_heads):
            folded = folded + mixture[:, kv_head * HEAD : (kv_head + 1) * HEAD]
        return folded

    copies[0][0].wait()
    weighed = [weigh(row) for row in groups[0]]
    for at in range(len(groups)):
        copies[at][1].wait()
        if at + 1 < len(groups):
            copies[at + 1][0].wait()
            following = [weigh(row) for row in groups[at + 1]]
        folded = [mix(row, *weighed[nth]) for nth, row in enumerate(groups[at])]
        mixed[...] = jnp.concatenate(folded, axis=0)
        share = [mixed[pl.ds(head, group, stride=head_count), :] for head in range(head_count)]
        share = jnp.concatenate(share, axis=1).astype(jnp.bfloat16)
        to_c, to_y = at // 2, at % 2
        for zx in range(8):
            out_ref[(1 - to_c) * 16 + to_y * 8 + zx] = share
        if at + 1 < len(groups):
            weighed = following


def attend_shares(queries, key_cache, value_cache, new_key, new_value, lengths):
    rows, width = queries.shape
    smem, hbm = pl.BlockSpec(memory_space=pltpu.SMEM), pl.BlockSpec(memory_space=pltpu.HBM)
    return pl.pallas_call(
        attend_kernel,
        out_shape=jax.ShapeDtypeStruct((32, 4, width), jnp.bfloat16),
        in_specs=[smem, *vmem(3), hbm, hbm],
        out_specs=pl.BlockSpec(memory_space=pltpu.VMEM),
        scratch_shapes=[
            pltpu.VMEM(key_cache.shape, key_cache.dtype),
            pltpu.VMEM(value_cache.shape, value_cache.dtype),
            pltpu.VMEM((rows * width // HEAD, HEAD), jnp.float32),
            pltpu.VMEM((4 * width // HEAD, HEAD), jnp.float32),
            pltpu.SemaphoreType.DMA((2, rows // 4)),
        ],
        compiler_params=pltpu.CompilerParams(vmem_limit_bytes=56 * 1024 * 1024),
        cost_estimate=cost(12e-6),
        name="attend",
    )(lengths, queries, new_key, new_value, key_cache, value_cache)


def keep_kernel(kept_own, kept_other, *rest):
    out_ref, _, turned = rest[-3:]
    y, c = lax.axis_index("y"), lax.axis_index("c")
    for at, kept in enumerate((kept_own, kept_other)):
        turned[...] = kept[...].astype(jnp.float32).T
        for b in range(turned.shape[0] // 16):
            both = turned[pl.ds(pl.multiple_of(b * 16 + 8 * c, 8), 8), :]
            out_ref[at, 4 * b : 4 * b + 4, :] = jnp.where(y == 0, both[:4], both[4:])


def keep(kept_own, kept_other, ready):
    features, rows = kept_own.shape
    return pl.pallas_call(
        keep_kernel,
        out_shape=(
            jax.ShapeDtypeStruct((2, rows // 4, features), jnp.float32),
            jax.ShapeDtypeStruct((8, 128), jnp.float32),
        ),
        in_specs=vmem(2) + [pl.BlockSpec(memory_space=pl.ANY)] * len(ready),
        out_specs=(*vmem(1), pl.BlockSpec(memory_space=pl.ANY)),
        scratch_shapes=[pltpu.VMEM((rows, features), jnp.float32)],
        compiler_params=pltpu.CompilerParams(vmem_limit_bytes=4 * 1024 * 1024),
        cost_estimate=cost(1e-6),
        name="keep",
    )(kept_own, kept_other, *ready)


def after(value, *others):
    def kernel(*refs):
        pass

    anywhere = pl.BlockSpec(memory_space=pl.ANY)
    return pl.pallas_call(
        kernel,
        out_shape=jax.ShapeDtypeStruct(value.shape, value.dtype),
        in_specs=[anywhere] * (1 + len(others)),
        out_specs=anywhere,
        input_output_aliases={0: 0},
        compiler_params=pltpu.CompilerParams(vmem_limit_bytes=1024 * 1024),
        name="after",
    )(value, *others)


def project_kernel(taken, near_own, near_other, far_own, kept, *rest):
    far_other, (out_ref, rows) = rest[:-2], rest[-2:]
    y, core = lax.axis_index("y"), lax.axis_index("c")
    blocks, share = taken.shape[0] // 2, taken.shape[1]
    for b in range(blocks):
        at = (1 - b % 2) * blocks + b // 2
        rows[0, b * share : (b + 1) * share, :] = taken[at + y * 8].astype(jnp.float32)
        rows[1, b * share : (b + 1) * share, :] = taken[at + (1 - y) * 8].astype(jnp.float32)
    near, far = rows[0].astype(jnp.bfloat16), rows[1].astype(jnp.bfloat16)

    def across(left, right):
        return lax.dot_general(left, right, ACROSS, preferred_element_type=jnp.float32)

    own = kept[0] + across(near, near_own[...]) + across(far, far_own[...])
    other = kept[1] + across(near, near_other[...])
    depth = far_other[0].shape[1]
    for at, piece in enumerate(far_other):
        other += across(far[:, at * depth : (at + 1) * depth], piece[...])
    first, second = jnp.where(core == 0, own, other), jnp.where(core == 0, other, own)
    stream = jnp.concatenate([first, second], axis=1).astype(jnp.bfloat16)
    half = stream.shape[0] // 2
    out_ref[0] = stream[:half]
    out_ref[1] = stream[half:]


def project(taken, near_own, near_other, far_own, far_other, kept):
    depth = taken.shape[2]
    rows, width = kept.shape[1:]
    return pl.pallas_call(
        project_kernel,
        out_shape=jax.ShapeDtypeStruct((2, rows // 2, 2 * width), jnp.bfloat16),
        in_specs=vmem(5 + len(far_other)),
        out_specs=pl.BlockSpec(memory_space=pltpu.VMEM),
        scratch_shapes=[pltpu.VMEM((2, rows, depth), jnp.float32)],
        compiler_params=pltpu.CompilerParams(vmem_limit_bytes=16 * 1024 * 1024),
        cost_estimate=cost(2e-6),
        name="project",
    )(taken, near_own, near_other, far_own, kept, *far_other)


def pre_activations(rows, weights):
    block = rows[0].shape[1]
    main = block // 256 * 256
    rest = jnp.concatenate([row[:, main:] for row in rows], axis=1)
    sums = []
    for half in range(2):
        total = None
        for dz, row in enumerate(rows):
            part = jnp.dot(row[:, :main], weights[half, dz, :main, :], preferred_element_type=jnp.float32)
            total = part if total is None else total + part
        ends = jnp.concatenate([weights[half, dz, main:, :] for dz in range(4)], axis=0)
        sums.append(total + jnp.dot(rest, ends, preferred_element_type=jnp.float32))
    return sums


def encode_first_kernel(own, other, own_far, other_far, enc_own, enc_other, out_ref, later_ref, weights, arrived):
    z, x = lax.axis_index("z"), lax.axis_index("x")
    block = own.shape[3]
    pairs = ((own, other), (own_far, other_far))
    now, later = [], []
    for half, enc in enumerate((enc_own, enc_other)):
        for dz in range(4):
            for dx, to, copies in ((0, weights, now), (1, later_ref, later)):
                start = pl.multiple_of(((z ^ dz) * 2 + (x ^ dx)) * block, 64)
                sem = arrived.at[dx, half * 4 + dz]
                copies.append(pltpu.make_async_copy(enc.at[pl.ds(start, block)], to.at[half, dz], sem))
    for copy in now + later:
        copy.start()
    for copy in now:
        copy.wait()
    rows = [
        jnp.concatenate([piece[half, dz] for piece in pair for half in range(2)], axis=0)
        for pair in pairs
        for dz in range(2)
    ]
    sums = pre_activations(rows, weights)
    out_ref[0] = sums[0]
    out_ref[1] = sums[1]
    for copy in later:
        copy.wait()


def encode_second_kernel(
    own,
    upper,
    lower,
    own_far,
    upper_far,
    lower_far,
    first,
    weights,
    bias_own,
    code_own,
    probe_own,
    bias_other,
    code_other,
    probe_other,
    out_ref,
    ordered,
):
    rows = [
        jnp.concatenate([piece[0, dz], piece[1, dz], up[dz], low[dz]], axis=0)
        for piece, up, low in ((own, upper, lower), (own_far, upper_far, lower_far))
        for dz in range(2)
    ]
    sums = pre_activations(rows, weights)
    partial = None
    halves = ((bias_own, code_own, probe_own), (bias_other, code_other, probe_other))
    for at, (bias, code, probe) in enumerate(halves):
        pre = sums[at] + first[at] + bias[...]
        threshold = code[...].astype(jnp.float32) / 16.0
        ramped = jnp.clip((pre - threshold) / RAMP_WIDTH, 0.0, 1.0)
        active = (pre * ramped).astype(jnp.bfloat16)
        probed = jnp.dot(active, probe[...], preferred_element_type=jnp.float32)
        partial = probed if partial is None else partial + probed
    for half in range(2):
        for b in range(16):
            at = half * 64 + b * 4
            ordered[15 - b, 4 * half : 4 * half + 4, :] = partial[at : at + 4, :]
    out_ref[...] = ordered[...].astype(jnp.bfloat16)


def encode_first(near, far, enc):
    own = near[0]
    rows, block, latents = 4 * own.shape[2], own.shape[3], enc[0].shape[1]
    weights = (2, 4, block, latents)
    hbm = pl.BlockSpec(memory_space=pltpu.HBM)
    return pl.pallas_call(
        encode_first_kernel,
        out_shape=(
            jax.ShapeDtypeStruct((2, rows, latents), jnp.float32),
            jax.ShapeDtypeStruct(weights, enc[0].dtype),
        ),
        in_specs=[*vmem(4), hbm, hbm],
        out_specs=tuple(vmem(2)),
        scratch_shapes=[pltpu.VMEM(weights, enc[0].dtype), pltpu.SemaphoreType.DMA((2, 8))],
        compiler_params=pltpu.CompilerParams(vmem_limit_bytes=50 * 1024 * 1024),
        cost_estimate=cost(2e-6),
        name="encode_first",
    )(*near, *far, *enc)


def encode_second(near, far, first, weights, own, other):
    columns = own[2].shape[1]
    return pl.pallas_call(
        encode_second_kernel,
        out_shape=jax.ShapeDtypeStruct((16, 8, columns), jnp.bfloat16),
        in_specs=vmem(14),
        out_specs=pl.BlockSpec(memory_space=pltpu.VMEM),
        scratch_shapes=[pltpu.VMEM((16, 8, columns), jnp.float32)],
        compiler_params=pltpu.CompilerParams(vmem_limit_bytes=24 * 1024 * 1024),
        cost_estimate=cost(2e-6),
        name="encode_second",
    )(*near, *far, first, weights, *own, *other)


def finish_kernel(parts, probe_bias, head_weight, head_bias, scores_ref, logits_ref):
    sums = parts[...].astype(jnp.float32)
    first = jnp.sum(sums[8:], axis=0)
    second = jnp.sum(sums[:8], axis=0)
    scores = first + jnp.concatenate([second[4:], second[:4]], axis=0) + probe_bias[...]
    scores_ref[...] = scores
    gated = scores / (1.0 + jnp.exp(-scores))
    logits_ref[...] = (
        lax.dot_general(
            gated,
            head_weight[...],
            (((1,), (1,)), ((), ())),
            precision=lax.Precision.HIGHEST,
            preferred_element_type=jnp.float32,
        )
        + head_bias[...]
    )


def finish(parts, probe_bias, head_weight, head_bias):
    rows, columns = parts.shape[1:]
    return pl.pallas_call(
        finish_kernel,
        out_shape=(
            jax.ShapeDtypeStruct((rows, columns), jnp.float32),
            jax.ShapeDtypeStruct((rows, head_weight.shape[1]), jnp.float32),
        ),
        in_specs=vmem(4),
        out_specs=tuple(vmem(2)),
        compiler_params=pltpu.CompilerParams(vmem_limit_bytes=8 * 1024 * 1024),
        name="finish",
    )(parts, probe_bias.reshape(1, -1), head_weight.T, head_bias.reshape(1, -1))


def chip_body(
    queries,
    key_cache,
    value_cache,
    new_key,
    new_value,
    lengths,
    out_proj,
    residual,
    enc_weight,
    enc_bias,
    threshold_code,
    probe_weight,
    probe_bias,
    head_weight,
    head_bias,
):
    proj = out_proj.T
    proj_y = xor(proj, 16)
    enc_other = xor(enc_weight, 1)
    proj_c = xor(proj, 1)
    probe_other = xor(probe_weight, 1)
    bias_other, code_other = xor(enc_bias, 1), xor(threshold_code, 1)
    kept = residual.T
    kept_other = xor(kept, 1)

    sent = attend_shares(queries, key_cache, value_cache, new_key, new_value, lengths)
    kept_rows, token = keep(kept, kept_other, ())
    taken = lax.all_to_all(sent, ALL, 0, 0, tiled=True, axis_index_groups=[ORDER])
    proj_y = after(proj_y, token)
    depth = proj_y.shape[1] // 4
    proj_yc = [xor(proj_y[:, at : at + depth], 1) for at in range(0, proj_y.shape[1], depth)]
    taken = after(taken, *proj_yc, probe_other, bias_other, code_other)
    stream = project(taken, proj, proj_c, proj_y, proj_yc, kept_rows)
    along_z = [stream, xor(stream, 4), xor(stream, 8), xor(stream, 12)]

    def spread(mine):
        over_y, over_x = xor(mine, 16), xor(mine, 2)
        return (mine, over_y), (over_x, xor(over_x[0], 16), xor(over_y[1], 2))

    first_near, second_near = spread(jnp.stack(along_z[:2], axis=1))
    first_far, second_far = spread(after(jnp.stack(along_z[2:], axis=1), second_near[0]))
    first, weights = encode_first(first_near, first_far, (enc_weight, enc_other))
    partial = encode_second(
        second_near,
        second_far,
        first,
        weights,
        (enc_bias[None], threshold_code[None], probe_weight),
        (bias_other[None], code_other[None], probe_other),
    )
    parts = lax.all_to_all(partial, ALL, 0, 0, tiled=True, axis_index_groups=PLANES)
    return finish(parts, probe_bias, head_weight, head_bias)


def body(
    queries,
    key_cache,
    value_cache,
    new_key,
    new_value,
    lengths,
    out_proj,
    residual,
    enc_weight,
    enc_bias,
    threshold_code,
    probe_weight,
    probe_bias,
    head_weight,
    head_bias,
):
    attended = attend(queries, key_cache, value_cache, new_key, new_value, lengths)
    partial_heads = jnp.dot(
        lax.all_gather(attended, "lat", axis=0, tiled=True),
        out_proj,
        preferred_element_type=jnp.float32,
    )
    projected = lax.psum(partial_heads, "tp")
    stream = (residual.astype(jnp.float32) + projected).astype(jnp.bfloat16)
    pre_act = jnp.dot(
        lax.all_gather(stream, "lat", axis=1, tiled=True),
        enc_weight,
        preferred_element_type=jnp.float32,
    )
    pre_act = pre_act + enc_bias
    threshold = threshold_code.astype(jnp.float32) / 16.0
    ramped = jnp.clip((pre_act - threshold) / RAMP_WIDTH, 0.0, 1.0)
    activations = (pre_act * ramped).astype(jnp.bfloat16)
    halfway = lax.psum_scatter(
        jnp.dot(activations, probe_weight, preferred_element_type=jnp.float32),
        "tp",
        scatter_dimension=0,
        tiled=True,
    )
    summed = lax.psum_scatter(halfway, "lat", scatter_dimension=0, tiled=True)
    probe_scores = summed + probe_bias
    harm_logits = (
        jnp.dot(
            jax.nn.silu(probe_scores),
            head_weight,
            precision=lax.Precision.HIGHEST,
            preferred_element_type=jnp.float32,
        )
        + head_bias
    )
    return (probe_scores, harm_logits)


def solution(mesh):
    chips = mesh.shape["tp"] == 2 and mesh.shape["lat"] == 16
    tp, lat = "tp", "lat"
    if chips:
        mesh = Mesh(mesh.devices.reshape(2, 4, 2, 2), ALL)
        tp, lat = ("y",), ("z", "x", "c")
    both = ALL if chips else ("tp", "lat")
    in_specs = (
        P(lat, tp),
        P(lat, None, tp),
        P(lat, None, tp),
        P(lat, tp),
        P(lat, tp),
        P(lat),
        P(tp, lat),
        P(None, lat),
        P(None, both),
        P(both),
        P(both),
        P(both, None),
        P(),
        P(),
        P(),
    )
    out_specs = (P(both, None), P(both, None))
    return jax.shard_map(
        chip_body if chips else body, mesh=mesh, in_specs=in_specs, out_specs=out_specs, check_vma=False
    )
```

```python
import jax
import jax.numpy as jnp
from jax import lax
from jax.experimental import pallas as pl
from jax.experimental.pallas import tpu as pltpu
from jax.sharding import Mesh, PartitionSpec as P

HEAD = 128


SOFT_CAP = 50.0
QUERY_SCALE = 1.0 / 12.0
RAMP_WIDTH = 0.25
ACROSS = (((1,), (1,)), ((), ()))

ALL = ("y", "z", "x", "c")
ORDER = [*range(1, 32, 2), *range(0, 32, 2)]
PLANES = [list(range(30 + core, -1, -2)) for core in range(2)]


def attend(queries, key_cache, value_cache, new_key, new_value, lengths):
    row_count, positions, kv_width = key_cache.shape
    kv_heads = kv_width // HEAD
    group_size = queries.shape[1] // kv_width
    grouped = queries.reshape(row_count, kv_heads, group_size, HEAD)
    key_rows = key_cache.reshape(row_count, positions, kv_heads, HEAD)
    values = value_cache.reshape(row_count, positions, kv_heads, HEAD)
    fresh_key = new_key.reshape(row_count, kv_heads, HEAD)
    fresh_value = new_value.reshape(row_count, kv_heads, 1, HEAD).astype(jnp.float32)
    cached = jnp.einsum("rkgd,rlkd->rkgl", grouped, key_rows, preferred_element_type=jnp.float32)
    own_score = jnp.einsum("rkgd,rkd->rkg", grouped, fresh_key, preferred_element_type=jnp.float32)
    cached = SOFT_CAP * jnp.tanh(cached * (QUERY_SCALE / SOFT_CAP))
    own_score = SOFT_CAP * jnp.tanh(own_score * (QUERY_SCALE / SOFT_CAP))
    live_mask = jnp.arange(positions, dtype=jnp.int32)[None, :] < lengths[:, None]
    cached_exp = jnp.where(live_mask[:, None, None, :], jnp.exp(cached), 0.0)
    own_exp = jnp.exp(own_score)
    denominator = jnp.sum(cached_exp, axis=-1) + own_exp
    cached_weight = (cached_exp / denominator[..., None]).astype(jnp.bfloat16)
    own_weight = (own_exp / denominator).astype(jnp.bfloat16)
    mixture = jnp.einsum(
        "rkgl,rlkd->rkgd", cached_weight, values, preferred_element_type=jnp.float32
    )
    mixture = mixture + own_weight.astype(jnp.float32)[..., None] * fresh_value
    return mixture.reshape(row_count, kv_heads * group_size * HEAD).astype(jnp.bfloat16)


def xor(value, bits):
    return lax.ppermute(value, ALL, [(i, i ^ bits) for i in range(32)])


def cost(seconds):
    return pl.CostEstimate(flops=0, bytes_accessed=int(seconds * 3.69e12), transcendentals=0)


def vmem(count):
    return [pl.BlockSpec(memory_space=pltpu.VMEM)] * count


def attend_kernel(
    lengths,
    queries,
    new_key,
    new_value,
    keys_at,
    values_at,
    out_ref,
    keys,
    values,
    heads,
    mixed,
    arrived,
):
    row_count, positions, kv_width = keys.shape
    head_count = queries.shape[1] // HEAD
    kv_heads = kv_width // HEAD
    group = 4
    groups = [range(at, at + group) for at in range(0, row_count, group)]
    copies = []
    for at in range(len(groups)):
        rows = pl.ds(at * group, group)
        copies.append(
            (
                pltpu.make_async_copy(keys_at.at[rows], keys.at[rows], arrived.at[0, at]),
                pltpu.make_async_copy(values_at.at[rows], values.at[rows], arrived.at[1, at]),
            )
        )
    copies[0][0].start()
    for at in range(len(groups)):
        if at + 1 < len(groups):
            copies[at + 1][0].start()
        copies[at][1].start()
    for head in range(head_count):
        heads[pl.ds(head, row_count, stride=head_count), :] = queries[:, head * HEAD : (head + 1) * HEAD].astype(
            jnp.float32
        )
    shape = (head_count, kv_width)
    of_head = lax.broadcasted_iota(jnp.int32, shape, 0) // (head_count // kv_heads)
    in_block = of_head == lax.broadcasted_iota(jnp.int32, shape, 1) // HEAD
    place = lax.broadcasted_iota(jnp.int32, (head_count, positions), 1)
    fresh_key = new_key[...].astype(jnp.float32)
    fresh_value = new_value[...].astype(jnp.float32)

    def cap(score):
        return jnp.exp(SOFT_CAP * jnp.tanh(score * (QUERY_SCALE / SOFT_CAP)))

    def weigh(row):
        query = heads[row * head_count : (row + 1) * head_count, :]
        spread = jnp.where(in_block, jnp.concatenate([query] * kv_heads, axis=1), 0.0)
        scores = lax.dot_general(
            spread.astype(jnp.bfloat16), keys[row], ACROSS, preferred_element_type=jnp.float32
        )
        own = cap(jnp.sum(spread * fresh_key[row : row + 1, :], axis=1, keepdims=True))
        exps = jnp.where(place < lengths[row], cap(scores), 0.0)
        scale = 1.0 / (jnp.sum(exps, axis=1, keepdims=True) + own)
        return (exps * scale).astype(jnp.bfloat16), (own * scale).astype(jnp.bfloat16).astype(jnp.float32)

    def mix(row, weights, own_weight):
        mixture = jnp.dot(weights, values[row], preferred_element_type=jnp.float32)
        mixture = jnp.where(in_block, mixture + own_weight * fresh_value[row : row + 1, :], 0.0)
        folded = mixture[:, :HEAD]
        for kv_head in range(1, kv_heads):
            folded = folded + mixture[:, kv_head * HEAD : (kv_head + 1) * HEAD]
        return folded

    copies[0][0].wait()
    weighed = [weigh(row) for row in groups[0]]
    for at in range(len(groups)):
        copies[at][1].wait()
        if at + 1 < len(groups):
            copies[at + 1][0].wait()
            following = [weigh(row) for row in groups[at + 1]]
        folded = [mix(row, *weighed[nth]) for nth, row in enumerate(groups[at])]
        mixed[...] = jnp.concatenate(folded, axis=0)
        share = [mixed[pl.ds(head, group, stride=head_count), :] for head in range(head_count)]
        share = jnp.concatenate(share, axis=1).astype(jnp.bfloat16)
        to_c, to_y = at // 2, at % 2
        for zx in range(8):
            out_ref[(1 - to_c) * 16 + to_y * 8 + zx] = share
        if at + 1 < len(groups):
            weighed = following


def attend_shares(queries, key_cache, value_cache, new_key, new_value, lengths):
    rows, width = queries.shape
    smem, hbm = pl.BlockSpec(memory_space=pltpu.SMEM), pl.BlockSpec(memory_space=pltpu.HBM)
    return pl.pallas_call(
        attend_kernel,
        out_shape=jax.ShapeDtypeStruct((32, 4, width), jnp.bfloat16),
        in_specs=[smem, *vmem(3), hbm, hbm],
        out_specs=pl.BlockSpec(memory_space=pltpu.VMEM),
        scratch_shapes=[
            pltpu.VMEM(key_cache.shape, key_cache.dtype),
            pltpu.VMEM(value_cache.shape, value_cache.dtype),
            pltpu.VMEM((rows * width // HEAD, HEAD), jnp.float32),
            pltpu.VMEM((4 * width // HEAD, HEAD), jnp.float32),
            pltpu.SemaphoreType.DMA((2, rows // 4)),
        ],
        compiler_params=pltpu.CompilerParams(vmem_limit_bytes=56 * 1024 * 1024),
        cost_estimate=cost(12e-6),
        name="attend",
    )(lengths, queries, new_key, new_value, key_cache, value_cache)


def keep_kernel(kept_own, kept_other, *rest):
    out_ref, _, turned = rest[-3:]
    y, c = lax.axis_index("y"), lax.axis_index("c")
    for at, kept in enumerate((kept_own, kept_other)):
        turned[...] = kept[...].astype(jnp.float32).T
        for b in range(turned.shape[0] // 16):
            both = turned[pl.ds(pl.multiple_of(b * 16 + 8 * c, 8), 8), :]
            out_ref[at, 4 * b : 4 * b + 4, :] = jnp.where(y == 0, both[:4], both[4:])


def keep(kept_own, kept_other, ready):
    features, rows = kept_own.shape
    return pl.pallas_call(
        keep_kernel,
        out_shape=(
            jax.ShapeDtypeStruct((2, rows // 4, features), jnp.float32),
            jax.ShapeDtypeStruct((8, 128), jnp.float32),
        ),
        in_specs=vmem(2) + [pl.BlockSpec(memory_space=pl.ANY)] * len(ready),
        out_specs=(*vmem(1), pl.BlockSpec(memory_space=pl.ANY)),
        scratch_shapes=[pltpu.VMEM((rows, features), jnp.float32)],
        compiler_params=pltpu.CompilerParams(vmem_limit_bytes=4 * 1024 * 1024),
        cost_estimate=cost(1e-6),
        name="keep",
    )(kept_own, kept_other, *ready)


def after(value, *others):
    def kernel(*refs):
        pass

    anywhere = pl.BlockSpec(memory_space=pl.ANY)
    return pl.pallas_call(
        kernel,
        out_shape=jax.ShapeDtypeStruct(value.shape, value.dtype),
        in_specs=[anywhere] * (1 + len(others)),
        out_specs=anywhere,
        input_output_aliases={0: 0},
        compiler_params=pltpu.CompilerParams(vmem_limit_bytes=1024 * 1024),
        name="after",
    )(value, *others)


def project_kernel(taken, near_own, near_other, far_own, kept, *rest):
    far_other, (out_ref, rows) = rest[:-2], rest[-2:]
    y, core = lax.axis_index("y"), lax.axis_index("c")
    blocks, share = taken.shape[0] // 2, taken.shape[1]
    for b in range(blocks):
        at = (1 - b % 2) * blocks + b // 2
        rows[0, b * share : (b + 1) * share, :] = taken[at + y * 8].astype(jnp.float32)
        rows[1, b * share : (b + 1) * share, :] = taken[at + (1 - y) * 8].astype(jnp.float32)
    near, far = rows[0].astype(jnp.bfloat16), rows[1].astype(jnp.bfloat16)

    def across(left, right):
        return lax.dot_general(left, right, ACROSS, preferred_element_type=jnp.float32)

    width, depth = near_own.shape[0], far_other[0].shape[1]
    both = across(near, jnp.concatenate([near_own[...], near_other[...]], axis=0))
    for at, piece in enumerate(far_other):
        part = slice(at * depth, (at + 1) * depth)
        both += across(far[:, part], jnp.concatenate([far_own[:, part], piece[...]], axis=0))
    own, other = kept[0] + both[:, :width], kept[1] + both[:, width:]
    first, second = jnp.where(core == 0, own, other), jnp.where(core == 0, other, own)
    stream = jnp.concatenate([first, second], axis=1).astype(jnp.bfloat16)
    half = stream.shape[0] // 2
    out_ref[0] = stream[:half]
    out_ref[1] = stream[half:]


def project(taken, near_own, near_other, far_own, far_other, kept):
    depth = taken.shape[2]
    rows, width = kept.shape[1:]
    return pl.pallas_call(
        project_kernel,
        out_shape=jax.ShapeDtypeStruct((2, rows // 2, 2 * width), jnp.bfloat16),
        in_specs=vmem(5 + len(far_other)),
        out_specs=pl.BlockSpec(memory_space=pltpu.VMEM),
        scratch_shapes=[pltpu.VMEM((2, rows, depth), jnp.float32)],
        compiler_params=pltpu.CompilerParams(vmem_limit_bytes=16 * 1024 * 1024),
        cost_estimate=cost(2e-6),
        name="project",
    )(taken, near_own, near_other, far_own, kept, *far_other)


def pre_activations(rows, weights):
    block = rows[0].shape[1]
    main = block // 256 * 256
    rest = jnp.concatenate([row[:, main:] for row in rows], axis=1)
    sums = []
    for half in range(2):
        total = None
        for dz, row in enumerate(rows):
            part = jnp.dot(row[:, :main], weights[half, dz, :main, :], preferred_element_type=jnp.float32)
            total = part if total is None else total + part
        ends = jnp.concatenate([weights[half, dz, main:, :] for dz in range(4)], axis=0)
        sums.append(total + jnp.dot(rest, ends, preferred_element_type=jnp.float32))
    return sums


def encode_first_kernel(own, other, own_far, other_far, enc_own, enc_other, out_ref, later_ref, weights, arrived):
    z, x = lax.axis_index("z"), lax.axis_index("x")
    block = own.shape[3]
    pairs = ((own, other), (own_far, other_far))
    now, later = [], []
    for half, enc in enumerate((enc_own, enc_other)):
        for dz in range(4):
            for dx, to, copies in ((0, weights, now), (1, later_ref, later)):
                start = pl.multiple_of(((z ^ dz) * 2 + (x ^ dx)) * block, 64)
                sem = arrived.at[dx, half * 4 + dz]
                copies.append(pltpu.make_async_copy(enc.at[pl.ds(start, block)], to.at[half, dz], sem))
    for copy in now + later:
        copy.start()
    for copy in now:
        copy.wait()
    rows = [
        jnp.concatenate([piece[half, dz] for piece in pair for half in range(2)], axis=0)
        for pair in pairs
        for dz in range(2)
    ]
    sums = pre_activations(rows, weights)
    out_ref[0] = sums[0]
    out_ref[1] = sums[1]
    for copy in later:
        copy.wait()


def encode_second_kernel(
    own,
    upper,
    lower,
    own_far,
    upper_far,
    lower_far,
    first,
    weights,
    bias_own,
    code_own,
    probe_own,
    bias_other,
    code_other,
    probe_other,
    out_ref,
    ordered,
):
    rows = [
        jnp.concatenate([piece[0, dz], piece[1, dz], up[dz], low[dz]], axis=0)
        for piece, up, low in ((own, upper, lower), (own_far, upper_far, lower_far))
        for dz in range(2)
    ]
    sums = pre_activations(rows, weights)
    partial = None
    halves = ((bias_own, code_own, probe_own), (bias_other, code_other, probe_other))
    for at, (bias, code, probe) in enumerate(halves):
        pre = sums[at] + first[at] + bias[...]
        threshold = code[...].astype(jnp.float32) / 16.0
        ramped = jnp.clip((pre - threshold) / RAMP_WIDTH, 0.0, 1.0)
        active = (pre * ramped).astype(jnp.bfloat16)
        probed = jnp.dot(active, probe[...], preferred_element_type=jnp.float32)
        partial = probed if partial is None else partial + probed
    for half in range(2):
        for b in range(16):
            at = half * 64 + b * 4
            ordered[15 - b, 4 * half : 4 * half + 4, :] = partial[at : at + 4, :]
    out_ref[...] = ordered[...].astype(jnp.bfloat16)


def encode_first(near, far, enc):
    own = near[0]
    rows, block, latents = 4 * own.shape[2], own.shape[3], enc[0].shape[1]
    weights = (2, 4, block, latents)
    hbm = pl.BlockSpec(memory_space=pltpu.HBM)
    return pl.pallas_call(
        encode_first_kernel,
        out_shape=(
            jax.ShapeDtypeStruct((2, rows, latents), jnp.float32),
            jax.ShapeDtypeStruct(weights, enc[0].dtype),
        ),
        in_specs=[*vmem(4), hbm, hbm],
        out_specs=tuple(vmem(2)),
        scratch_shapes=[pltpu.VMEM(weights, enc[0].dtype), pltpu.SemaphoreType.DMA((2, 8))],
        compiler_params=pltpu.CompilerParams(vmem_limit_bytes=50 * 1024 * 1024),
        cost_estimate=cost(2e-6),
        name="encode_first",
    )(*near, *far, *enc)


def encode_second(near, far, first, weights, own, other):
    columns = own[2].shape[1]
    return pl.pallas_call(
        encode_second_kernel,
        out_shape=jax.ShapeDtypeStruct((16, 8, columns), jnp.bfloat16),
        in_specs=vmem(14),
        out_specs=pl.BlockSpec(memory_space=pltpu.VMEM),
        scratch_shapes=[pltpu.VMEM((16, 8, columns), jnp.float32)],
        compiler_params=pltpu.CompilerParams(vmem_limit_bytes=24 * 1024 * 1024),
        cost_estimate=cost(2e-6),
        name="encode_second",
    )(*near, *far, first, weights, *own, *other)


def finish_kernel(parts, probe_bias, head_weight, head_bias, scores_ref, logits_ref):
    sums = parts[...].astype(jnp.float32)
    first = jnp.sum(sums[8:], axis=0)
    second = jnp.sum(sums[:8], axis=0)
    scores = first + jnp.concatenate([second[4:], second[:4]], axis=0) + probe_bias[...]
    scores_ref[...] = scores
    gated = scores / (1.0 + jnp.exp(-scores))
    logits_ref[...] = (
        lax.dot_general(
            gated,
            head_weight[...],
            (((1,), (1,)), ((), ())),
            precision=lax.Precision.HIGHEST,
            preferred_element_type=jnp.float32,
        )
        + head_bias[...]
    )


def finish(parts, probe_bias, head_weight, head_bias):
    rows, columns = parts.shape[1:]
    return pl.pallas_call(
        finish_kernel,
        out_shape=(
            jax.ShapeDtypeStruct((rows, columns), jnp.float32),
            jax.ShapeDtypeStruct((rows, head_weight.shape[1]), jnp.float32),
        ),
        in_specs=vmem(4),
        out_specs=tuple(vmem(2)),
        compiler_params=pltpu.CompilerParams(vmem_limit_bytes=8 * 1024 * 1024),
        name="finish",
    )(parts, probe_bias.reshape(1, -1), head_weight.T, head_bias.reshape(1, -1))


def chip_body(
    queries,
    key_cache,
    value_cache,
    new_key,
    new_value,
    lengths,
    out_proj,
    residual,
    enc_weight,
    enc_bias,
    threshold_code,
    probe_weight,
    probe_bias,
    head_weight,
    head_bias,
):
    proj = out_proj.T
    proj_y = xor(proj, 16)
    enc_other = xor(enc_weight, 1)
    proj_c = xor(proj, 1)
    probe_other = xor(probe_weight, 1)
    bias_other, code_other = xor(enc_bias, 1), xor(threshold_code, 1)
    kept = residual.T
    kept_other = xor(kept, 1)

    sent = attend_shares(queries, key_cache, value_cache, new_key, new_value, lengths)
    kept_rows, token = keep(kept, kept_other, ())
    taken = lax.all_to_all(sent, ALL, 0, 0, tiled=True, axis_index_groups=[ORDER])
    proj_y = after(proj_y, token)
    depth = proj_y.shape[1] // 4
    proj_yc = [xor(proj_y[:, at : at + depth], 1) for at in range(0, proj_y.shape[1], depth)]
    taken = after(taken, *proj_yc, probe_other, bias_other, code_other)
    stream = project(taken, proj, proj_c, proj_y, proj_yc, kept_rows)
    along_z = [stream, xor(stream, 4), xor(stream, 8), xor(stream, 12)]

    def spread(mine):
        over_y, over_x = xor(mine, 16), xor(mine, 2)
        return (mine, over_y), (over_x, xor(over_x[0], 16), xor(over_y[1], 2))

    first_near, second_near = spread(jnp.stack(along_z[:2], axis=1))
    first_far, second_far = spread(after(jnp.stack(along_z[2:], axis=1), second_near[0]))
    first, weights = encode_first(first_near, first_far, (enc_weight, enc_other))
    partial = encode_second(
        second_near,
        second_far,
        first,
        weights,
        (enc_bias[None], threshold_code[None], probe_weight),
        (bias_other[None], code_other[None], probe_other),
    )
    parts = lax.all_to_all(partial, ALL, 0, 0, tiled=True, axis_index_groups=PLANES)
    return finish(parts, probe_bias, head_weight, head_bias)


def body(
    queries,
    key_cache,
    value_cache,
    new_key,
    new_value,
    lengths,
    out_proj,
    residual,
    enc_weight,
    enc_bias,
    threshold_code,
    probe_weight,
    probe_bias,
    head_weight,
    head_bias,
):
    attended = attend(queries, key_cache, value_cache, new_key, new_value, lengths)
    partial_heads = jnp.dot(
        lax.all_gather(attended, "lat", axis=0, tiled=True),
        out_proj,
        preferred_element_type=jnp.float32,
    )
    projected = lax.psum(partial_heads, "tp")
    stream = (residual.astype(jnp.float32) + projected).astype(jnp.bfloat16)
    pre_act = jnp.dot(
        lax.all_gather(stream, "lat", axis=1, tiled=True),
        enc_weight,
        preferred_element_type=jnp.float32,
    )
    pre_act = pre_act + enc_bias
    threshold = threshold_code.astype(jnp.float32) / 16.0
    ramped = jnp.clip((pre_act - threshold) / RAMP_WIDTH, 0.0, 1.0)
    activations = (pre_act * ramped).astype(jnp.bfloat16)
    halfway = lax.psum_scatter(
        jnp.dot(activations, probe_weight, preferred_element_type=jnp.float32),
        "tp",
        scatter_dimension=0,
        tiled=True,
    )
    summed = lax.psum_scatter(halfway, "lat", scatter_dimension=0, tiled=True)
    probe_scores = summed + probe_bias
    harm_logits = (
        jnp.dot(
            jax.nn.silu(probe_scores),
            head_weight,
            precision=lax.Precision.HIGHEST,
            preferred_element_type=jnp.float32,
        )
        + head_bias
    )
    return (probe_scores, harm_logits)


def solution(mesh):
    chips = mesh.shape["tp"] == 2 and mesh.shape["lat"] == 16
    tp, lat = "tp", "lat"
    if chips:
        mesh = Mesh(mesh.devices.reshape(2, 4, 2, 2), ALL)
        tp, lat = ("y",), ("z", "x", "c")
    both = ALL if chips else ("tp", "lat")
    in_specs = (
        P(lat, tp),
        P(lat, None, tp),
        P(lat, None, tp),
        P(lat, tp),
        P(lat, tp),
        P(lat),
        P(tp, lat),
        P(None, lat),
        P(None, both),
        P(both),
        P(both),
        P(both, None),
        P(),
        P(),
        P(),
    )
    out_specs = (P(both, None), P(both, None))
    return jax.shard_map(
        chip_body if chips else body, mesh=mesh, in_specs=in_specs, out_specs=out_specs, check_vma=False
    )
```
